256 devices in a mesh: seq: 4 (over x), batch: 64 (over y, z, core).
Axes of the slice: x: 4, y: 4, z: 8, core: 2. Of those that a mesh axis runs over, the one named last changes fastest.
Arguments:
- history: bfloat16 [64, 512, 512], P('batch', 'seq'), may hold values from -6 to 6
- out_cotangent: bfloat16 [64, 512, 512], P('batch', 'seq'), may hold values from -6 to 6
- lengths: int32 [64], P('batch'), may hold values from 1 to 512, as said below
- bucket_of: int32 [512], replicated, may hold values from 0 to 127, as said below
- position_bias: float32 [4, 128], replicated, may hold values from -4 to 4
- norm_gain: float32 [512], replicated, may hold values from 0.1 to 1.9
- uvqk_weight: bfloat16 [512, 2048], replicated, may hold values from -0.25 to 0.25
- out_gain: float32 [512], replicated, may hold values from 0.1 to 1.9
- out_weight: bfloat16 [512, 512], replicated, may hold values from -0.25 to 0.25
Outputs:
- output: bfloat16 [64, 512, 512], P('batch', 'seq')
- grad_input: bfloat16 [64, 512, 512], P('batch', 'seq')
- grad_uvqk_weight: float32 [512, 2048], replicated
- grad_out_weight: float32 [512, 512], replicated
- grad_position_bias: float32 [4, 128], replicated
- grad_norm_gain: float32 [512], replicated
- grad_out_gain: float32 [512], replicated
The draws below stay inside these ranges and needn't reach their ends.
Inputs may be any that keep to these rules, and one draw needn't show every extreme that they name: `lengths`: one history in every draw has length exactly 512. `bucket_of`: nondecreasing in the distance, 0 at distance 0 and 127 at distance 512 - 1.
All inputs are finite; a program needn't handle non-finite values.
Results may differ from the reference program's by a relative error of at most 0.0082.
Values may be sent and summed in bfloat16 or wider, within the bound.
No kernel may reach another device: no remote copies, remote signals or barrier semaphores. Data moves between devices by JAX's collectives and lax.ppermute only.
A program may use at most 128 MiB of HBM per device.

```python
import math
import jax
import jax.numpy as jnp
from jax import lax

D = 512
HEADS = 4
NB = 128
SEQ = 512
HISTORIES = 64


def draw_lengths(key, part):
    key = jax.random.fold_in(key, 11)
    first_key, second_key, third_key = jax.random.split(key, 3)
    first_draw = jax.random.randint(first_key, (HISTORIES,), 1, SEQ + 1)
    second_draw = jax.random.randint(second_key, (HISTORIES,), 1, SEQ + 1)
    longest = jax.random.randint(third_key, (), 0, HISTORIES)
    shortest = jnp.minimum(first_draw, second_draw)
    return shortest.at[longest].set(SEQ).astype(jnp.int32)


def draw_bucket_of(key, part):
    key = jax.random.fold_in(key, 23)
    raw_ids = jax.random.randint(key, (SEQ,), 0, NB)
    ordered = jnp.sort(raw_ids)
    return ordered.at[0].set(0).at[SEQ - 1].set(NB - 1).astype(jnp.int32)


def steps_of(stream_key, extent, pieces, least, top_value):
    def one(dim, shards_of):
        draws = jax.random.uniform(jax.random.fold_in(jax.random.fold_in(stream_key, 6), dim), (shards_of,), jnp.float32, least / len(pieces), top_value / len(pieces))
        return jnp.repeat(jnp.exp(draws), extent[dim] // shards_of).reshape((-1,) + (1,) * (len(extent) - dim - 1))

    loudness = one(*pieces[0])
    for cut in pieces[1:]:
        loudness = loudness * one(*cut)
    return loudness


def noise(own_key, shape, deviation, limit, cuts=(), held_as=jnp.bfloat16):
    array = deviation * jax.random.normal(own_key, shape, jnp.float32)
    if cuts:
        array = array * steps_of(own_key, shape, cuts, -0.22, 0.18)
    return jnp.clip(array, -limit, limit).astype(held_as)


def setup_inputs(seed: int = 0) -> dict:
    key_list = jax.random.split(jax.random.key(seed), 10)
    return {
        "history": noise(key_list[0], (HISTORIES, SEQ, D), 1.0, 6.0, ((0, 64), (1, 4))),
        "out_cotangent": noise(key_list[1], (HISTORIES, SEQ, D), 1.0, 6.0, ((0, 64), (1, 4))),
        "lengths": draw_lengths(jax.random.fold_in(key_list[9], 71), 0),
        "bucket_of": draw_bucket_of(jax.random.fold_in(key_list[9], 71), 0),
        "position_bias": noise(key_list[4], (HEADS, NB), 1.0, 4.0, (), jnp.float32),
        "norm_gain": jnp.clip(1.0 + 0.18 * jax.random.normal(key_list[5], (D,), jnp.float32), 0.1, 1.9),
        "uvqk_weight": noise(key_list[6], (D, 4 * D), D ** -0.5, 0.25),
        "out_gain": jnp.clip(1.0 + 0.18 * jax.random.normal(key_list[7], (D,), jnp.float32), 0.1, 1.9),
        "out_weight": noise(key_list[8], (D, D), D ** -0.5, 0.25),
    }


NORM_EPS = 1e-05

def normalize(values):
    centered = values - lax.optimization_barrier(jnp.mean(values, axis=-1, keepdims=True))
    inv_scale = lax.rsqrt(lax.optimization_barrier(jnp.mean(centered * centered, axis=-1, keepdims=True)) + NORM_EPS)
    return (centered * inv_scale, inv_scale)

def silu_slope(values):
    sigmoid = jax.nn.sigmoid(values)
    return sigmoid * (1.0 + values * (1.0 - sigmoid))

def norm_backward(grad_normed, normed, inv_scale):
    return inv_scale * (grad_normed - lax.optimization_barrier(jnp.mean(grad_normed, axis=-1, keepdims=True)) - normed * lax.optimization_barrier(jnp.mean(grad_normed * normed, axis=-1, keepdims=True)))

def one_history(history, out_cotangent, length, bucket_of, bias_by_distance, norm_gain, uvqk_weight, out_gain, out_weight):
    head_dim = D // HEADS
    score_scale = 1.0 / math.sqrt(head_dim)
    history_wide = history.astype(jnp.float32)
    normed, inv_in = normalize(history_wide)
    scaled_low = (normed * norm_gain).astype(jnp.bfloat16)
    projected = jnp.dot(scaled_low, uvqk_weight, preferred_element_type=jnp.float32)
    activated = jax.nn.silu(projected)
    gating = activated[:, :D]
    value_low = activated[:, D:2 * D].astype(jnp.bfloat16)
    query_low = activated[:, 2 * D:3 * D].astype(jnp.bfloat16)
    key_low = activated[:, 3 * D:].astype(jnp.bfloat16)
    position = jnp.arange(SEQ, dtype=jnp.int32)
    visible = (position[None, :] <= position[:, None]) & (position[:, None] < length)
    distance = jnp.clip(position[:, None] - position[None, :], 0, SEQ - 1).astype(jnp.int32)
    query_heads = query_low.astype(jnp.float32).reshape(SEQ, HEADS, head_dim)
    key_heads = key_low.astype(jnp.float32).reshape(SEQ, HEADS, head_dim)
    value_heads = value_low.astype(jnp.float32).reshape(SEQ, HEADS, head_dim)
    scores = jnp.einsum('ihd,jhd->hij', query_heads, key_heads) * score_scale + bias_by_distance[:, distance]
    weights_low = jnp.where(visible[None], jax.nn.silu(scores), 0.0).astype(jnp.bfloat16)
    weights_wide = weights_low.astype(jnp.float32)
    mixed = jnp.einsum('hij,jhd->ihd', weights_wide, value_heads).reshape(SEQ, D)
    mixed_normed, inv_mixed = normalize(mixed)
    gated_low = (mixed_normed * out_gain * gating).astype(jnp.bfloat16)
    output = (history_wide + jnp.dot(gated_low, out_weight, preferred_element_type=jnp.float32)).astype(jnp.bfloat16)
    grad_out_weight = jnp.dot(gated_low.T, out_cotangent, preferred_element_type=jnp.float32)
    grad_gated = jnp.dot(out_cotangent, out_weight.T, preferred_element_type=jnp.float32)
    grad_out_gain = lax.optimization_barrier(jnp.sum(grad_gated * mixed_normed * gating, axis=0))
    grad_gating = grad_gated * mixed_normed * out_gain
    grad_mixed_low = norm_backward(grad_gated * out_gain * gating, mixed_normed, inv_mixed).astype(jnp.bfloat16)
    grad_heads = grad_mixed_low.astype(jnp.float32).reshape(SEQ, HEADS, head_dim)
    grad_weights = jnp.einsum('ihd,jhd->hij', grad_heads, value_heads)
    grad_scores = jnp.where(visible[None], grad_weights * silu_slope(scores), 0.0)
    grad_scores_wide = grad_scores.astype(jnp.bfloat16).astype(jnp.float32)
    grad_query = jnp.einsum('hij,jhd->ihd', grad_scores_wide, key_heads).reshape(SEQ, D) * score_scale
    grad_key = jnp.einsum('hij,ihd->jhd', grad_scores_wide, query_heads).reshape(SEQ, D) * score_scale
    grad_value = jnp.einsum('hij,ihd->jhd', weights_wide, grad_heads).reshape(SEQ, D)
    bucket_ids = bucket_of[distance].reshape(-1)
    grad_bias = jax.ops.segment_sum(grad_scores.reshape(HEADS, SEQ * SEQ).T, bucket_ids, num_segments=NB).T
    grad_projected_low = (jnp.concatenate([grad_gating, grad_value, grad_query, grad_key], axis=1) * silu_slope(projected)).astype(jnp.bfloat16)
    grad_uvqk = jnp.dot(scaled_low.T, grad_projected_low, preferred_element_type=jnp.float32)
    grad_scaled = jnp.dot(grad_projected_low, uvqk_weight.T, preferred_element_type=jnp.float32)
    grad_norm_gain = lax.optimization_barrier(jnp.sum(grad_scaled * normed, axis=0))
    grad_input = (out_cotangent.astype(jnp.float32) + norm_backward(grad_scaled * norm_gain, normed, inv_in)).astype(jnp.bfloat16)
    return (output, grad_input, (grad_uvqk, grad_out_weight, grad_bias, grad_norm_gain, grad_out_gain))

def reference(history, out_cotangent, lengths, bucket_of, position_bias, norm_gain, uvqk_weight, out_gain, out_weight):
    bias_by_distance = position_bias[:, bucket_of]
    initial = (jnp.zeros((D, 4 * D), jnp.float32), jnp.zeros((D, D), jnp.float32), jnp.zeros((HEADS, NB), jnp.float32), jnp.zeros((D,), jnp.float32), jnp.zeros((D,), jnp.float32))

    def advance(running, item):
        history_one, cotangent_one, length_one = item
        output, grad_input, grads = one_history(history_one, cotangent_one, length_one, bucket_of, bias_by_distance, norm_gain, uvqk_weight, out_gain, out_weight)
        return (jax.tree.map(lambda left, right: left + right, running, grads), (output, grad_input))
    totals, (outputs, grad_inputs) = lax.scan(advance, initial, (history, out_cotangent, lengths))
    factor = 1.0 / math.sqrt(HISTORIES * SEQ)
    return (outputs, grad_inputs, totals[0] * factor, totals[1] * factor, totals[2] * factor, totals[3] * factor, totals[4] * factor)
```

```python
import functools
import math

import jax
import jax.numpy as jnp
from jax import lax
from jax.experimental import pallas as pl
from jax.experimental.pallas import tpu as pltpu
from jax.sharding import PartitionSpec as P

NORM_EPS = 1e-05
BF = jnp.bfloat16
F32 = jnp.float32
VMEM_LIMIT = 56 * 1024 * 1024
HIDDEN = -1e9


def normalize(values):
    centered = values - jnp.mean(values, axis=-1, keepdims=True)
    inv_scale = lax.rsqrt(jnp.mean(centered * centered, axis=-1, keepdims=True) + NORM_EPS)
    return (centered * inv_scale, inv_scale)


def norm_backward(grad_normed, normed, inv_scale):
    return inv_scale * (
        grad_normed
        - jnp.mean(grad_normed, axis=-1, keepdims=True)
        - normed * jnp.mean(grad_normed * normed, axis=-1, keepdims=True)
    )


def sigmoid(values):
    return 0.5 * jnp.tanh(0.5 * values) + 0.5


def dot_nn(left, right):
    return lax.dot_general(left, right, (((1,), (0,)), ((), ())), preferred_element_type=F32)


def dot_nt(left, right):
    return lax.dot_general(left, right, (((1,), (1,)), ((), ())), preferred_element_type=F32)


def dot_tn(left, right):
    return lax.dot_general(left, right, (((0,), (0,)), ((), ())), preferred_element_type=F32)


def three_parts(values):
    high = values.astype(BF)
    rest = values - high.astype(F32)
    middle = rest.astype(BF)
    low = (rest - middle.astype(F32)).astype(BF)
    return high, middle, low


def as_rows(row, parts):
    width = row.shape[1] // parts
    return jnp.concatenate([row[:, p * width : (p + 1) * width] for p in range(parts)], axis=0)


def layer_kernel(
    seq_size,
    length_ref,
    own_ref,
    own_cot_ref,
    *refs,
):
    pieces = refs[: seq_size - 1]
    (
        bucket_ref,
        bias_ref,
        in_gain_ref,
        uvqk_ref,
        out_gain_ref,
        out_w_ref,
        output_ref,
        grad_input_ref,
        send_ref,
        keep_ref,
        hist_s,
        cot_s,
        scaled_s,
        gate_s,
        slope_s,
        vqk_s,
        tile_s,
        gated_s,
        weights_s,
        grads_s,
        score_slope_s,
        grad_mixed_s,
        proj_grad_s,
        diag_s,
    ) = refs[seq_size - 1 :]
    rows, width = own_ref.shape
    total = rows * seq_size
    heads, buckets = bias_ref.shape
    head_dim = width // heads
    scale = 1.0 / math.sqrt(head_dim)
    me = lax.axis_index("seq")
    core = lax.rem(lax.axis_index("batch"), 2)
    length = length_ref[0]
    own_rows = pl.ds(pl.multiple_of(me * rows, rows), rows)

    hist_s[own_rows, :] = own_ref[...]
    cot_s[own_rows, :] = own_cot_ref[...]
    for step, piece in zip((1, 3, 2), pieces):
        source = lax.rem(me + seq_size - step, seq_size)
        place = pl.ds(pl.multiple_of(source * rows, rows), rows)
        hist_s[place, :] = piece[:, :width]
        cot_s[place, :] = piece[:, width:]

    span = total + rows
    offset = total - rows
    turned = offset - lax.broadcasted_iota(jnp.int32, (total, span), 1)
    turned = jnp.where(turned < 0, turned + span, turned)
    pick = (lax.broadcasted_iota(jnp.int32, (total, span), 0) == turned).astype(F32).astype(BF)
    bucket_rows = jnp.broadcast_to(bucket_ref[...].astype(F32), (8, total)).astype(BF)
    bucket_row = dot_nn(bucket_rows, pick)[:1, :]
    column = offset - lax.broadcasted_iota(jnp.int32, (1, span), 1)
    seen = jnp.where(column < 0, column + span, column) < total
    bucket_row = jnp.where(seen, bucket_row, -1.0)
    onehot = (
        lax.broadcasted_iota(jnp.int32, (buckets, span), 0).astype(F32)
        == jnp.broadcast_to(bucket_row, (buckets, span))
    ).astype(F32).astype(BF)
    bias_rows = jnp.concatenate([bias_ref[...], jnp.zeros((8 - heads, buckets), F32)], axis=0)
    by_distance = sum(dot_nn(part, onehot) for part in three_parts(bias_rows))
    by_distance = jnp.where(seen, by_distance, HIDDEN)
    for h in range(heads):
        skewed = pltpu.roll(
            jnp.broadcast_to(by_distance[h : h + 1, :], (rows, span)), 0, 1, stride=1, stride_axis=0
        )
        tile_s[h] = skewed[:, :total]
        diag_s[h] = jnp.zeros((rows, total), F32)

    in_gain = in_gain_ref[...]
    out_gain = out_gain_ref[...]
    grad_out_gain = jnp.zeros((1, width), F32)

    for i in range(seq_size):
        here = slice(i * rows, (i + 1) * rows)
        ends = (i + 1) * rows
        first = total - ends
        normed, _ = normalize(hist_s[here, :].astype(F32))
        scaled = (normed * in_gain).astype(BF)
        scaled_s[here, :] = scaled
        for part in range(4):
            projected = dot_nn(scaled, uvqk_ref[:, part * width : (part + 1) * width])
            sig = sigmoid(projected)
            activated = projected * sig
            slope_s[part, here, :] = sig + activated * (1.0 - sig)
            if part == 0:
                gate_s[here, :] = activated
            else:
                vqk_s[part - 1, here, :] = activated.astype(BF)
        mixed_parts = []
        for h in range(heads):
            lanes = slice(h * head_dim, (h + 1) * head_dim)
            scores = dot_nt(vqk_s[1, here, lanes], vqk_s[2, :ends, lanes]) * scale
            scores = scores + tile_s[h, :, first:]
            sig = sigmoid(scores)
            weights = scores * sig
            score_slope_s[h, :, :ends] = sig + weights * (1.0 - sig)
            weights_low = weights.astype(BF)
            weights_s[h, here, :ends] = weights_low
            mixed_parts.append(dot_nn(weights_low, vqk_s[0, :ends, lanes]))
        valid = (lax.broadcasted_iota(jnp.int32, (rows, 1), 0) + i * rows) < length
        mixed = jnp.where(valid, jnp.concatenate(mixed_parts, axis=1), 0.0)
        mixed_normed, inv_mixed = normalize(mixed)
        gating = gate_s[here, :]
        gated_s[here, :] = (mixed_normed * out_gain * gating).astype(BF)
        grad_gated = dot_nt(cot_s[here, :], out_w_ref[...])
        times_normed = grad_gated * mixed_normed
        grad_out_gain = grad_out_gain + jnp.sum(times_normed * gating, axis=0, keepdims=True)
        proj_grad_s[0, here, :] = (times_normed * out_gain * slope_s[0, here, :]).astype(BF)
        grad_mixed = norm_backward(grad_gated * out_gain * gating, mixed_normed, inv_mixed)
        grad_mixed_low = jnp.where(valid, grad_mixed, 0.0).astype(BF)
        grad_mixed_s[here, :] = grad_mixed_low
        for h in range(heads):
            lanes = slice(h * head_dim, (h + 1) * head_dim)
            grad_weights = dot_nt(grad_mixed_low[:, lanes], vqk_s[0, :ends, lanes])
            grad_scores = grad_weights * score_slope_s[h, :, :ends]
            diag_s[h, :, first:] += grad_scores
            grad_scores_low = grad_scores.astype(BF)
            grads_s[h, here, :ends] = grad_scores_low
            grad_query = dot_nn(grad_scores_low, vqk_s[2, :ends, lanes]) * scale
            proj_grad_s[2, here, lanes] = (grad_query * slope_s[2, here, lanes]).astype(BF)

    for j in range(seq_size):
        here = slice(j * rows, (j + 1) * rows)
        later = slice(j * rows, total)
        for h in range(heads):
            lanes = slice(h * head_dim, (h + 1) * head_dim)
            grad_key = dot_tn(grads_s[h, later, here], vqk_s[1, later, lanes]) * scale
            proj_grad_s[3, here, lanes] = (grad_key * slope_s[3, here, lanes]).astype(BF)
            grad_value = dot_tn(weights_s[h, later, here], grad_mixed_s[later, lanes])
            proj_grad_s[1, here, lanes] = (grad_value * slope_s[1, here, lanes]).astype(BF)

    half = total // 2
    block = width // 4
    own_block = proj_grad_s[me]
    cot_block = cot_s[:, pl.ds(pl.multiple_of(me * block, block), block)]
    for ref, side in ((send_ref, 1 - core), (keep_ref, core)):
        lanes = pl.ds(pl.multiple_of(side * half, half), half)
        uvqk_term = dot_tn(scaled_s[:, lanes], own_block)
        for b in range(4):
            ref[b * half : (b + 1) * half, :] = uvqk_term[:, b * block : (b + 1) * block].astype(
                ref.dtype
            )
        out_term = dot_tn(gated_s[:, lanes], cot_block)
        ref[4 * half : 5 * half, :] = out_term.astype(ref.dtype)

    normed, inv_in = normalize(hist_s[own_rows, :].astype(F32))
    grad_scaled = jnp.zeros((rows, width), F32)
    for part in range(4):
        grad_scaled = grad_scaled + dot_nt(
            proj_grad_s[part, own_rows, :], uvqk_ref[:, part * width : (part + 1) * width]
        )
    grad_in_gain = jnp.sum(grad_scaled * normed, axis=0, keepdims=True)
    grad_input = cot_s[own_rows, :].astype(F32) + norm_backward(
        grad_scaled * in_gain, normed, inv_in
    )
    grad_input_ref[...] = grad_input.astype(BF)
    output = hist_s[own_rows, :].astype(F32) + dot_nn(gated_s[own_rows, :], out_w_ref[...])
    output_ref[...] = output.astype(BF)

    bias_sums = []
    for h in range(heads):
        folded = jnp.concatenate([diag_s[h], jnp.zeros((rows, span - total), F32)], axis=1)
        count = rows // 2
        while count >= 8:
            folded = folded[:count, :] + pltpu.roll(folded[count:, :], span - count, 1)
            count //= 2
        while count >= 1:
            folded = folded + pltpu.roll(pltpu.roll(folded, 8 - count, 0), span - count, 1)
            count //= 2
        bias_sums.append(folded[:1, :])
    bias_sums = jnp.concatenate(bias_sums + [jnp.zeros((8 - heads, span), F32)], axis=0)
    grad_bias = sum(dot_nt(part, onehot) for part in three_parts(bias_sums))[:heads, :]
    small = jnp.concatenate(
        [
            grad_bias,
            as_rows(grad_in_gain, 4),
            as_rows(grad_out_gain, 4),
            jnp.zeros((4, buckets), F32),
        ],
        axis=0,
    )
    row = lax.broadcasted_iota(jnp.int32, small.shape, 0)
    mine = (row == me) | ((row >= 4) & (row < 8)) | (row == 8 + me)
    small = jnp.where(mine, small, 0.0)
    send_ref[5 * half :, :] = small.astype(BF)
    keep_ref[5 * half :, :] = small


def after_core_kernel(keep_ref, got_ref, own_ref, one_ref, three_ref, two_ref):
    body = keep_ref.shape[0] - 16
    half = body // 5
    part = half // 4
    y = lax.axis_index("batch") // (lax.axis_size("batch") // 4)
    small = keep_ref[body:, :].astype(BF).astype(F32) + got_ref[body:, :].astype(F32)
    for ref, step in ((own_ref, 0), (one_ref, 1), (three_ref, 3), (two_ref, 2)):
        there = lax.rem(y + step, 4)
        for b in range(5):
            place = pl.ds(pl.multiple_of(b * half + there * part, part), part)
            ref[b * part : (b + 1) * part, :] = (
                keep_ref[place, :] + got_ref[place, :].astype(F32)
            ).astype(ref.dtype)
        ref[5 * part :, :] = small.astype(ref.dtype)


def after_y_kernel(own_ref, one_ref, three_ref, two_ref, sum_ref):
    body = own_ref.shape[0] - 16
    got = lambda ref, place: ref[place, :].astype(F32)
    for place, own in (
        (slice(0, body), own_ref[:body, :]),
        (slice(body, None), own_ref[body:, :].astype(BF).astype(F32)),
    ):
        sum_ref[place, :] = (
            (own + got(two_ref, place)) + (got(one_ref, place) + got(three_ref, place))
        ).astype(BF)


def pair_sum_kernel(left_ref, right_ref, sum_ref):
    sum_ref[...] = (left_ref[...].astype(F32) + right_ref[...].astype(F32)).astype(BF)


def ring_sum_kernel(own_ref, two_ref, six_ref, four_ref, sum_ref):
    sum_ref[...] = (
        (own_ref[...].astype(F32) + four_ref[...].astype(F32))
        + (two_ref[...].astype(F32) + six_ref[...].astype(F32))
    ).astype(BF)


def after_x_kernel(
    factor, own_ref, one_ref, three_ref, two_ref, all_ref, bias_ref, in_gain_ref, out_gain_ref
):
    body = own_ref.shape[0] - 16
    me = lax.axis_index("seq")
    for ref, step in ((own_ref, 0), (one_ref, 1), (three_ref, 3), (two_ref, 2)):
        source = lax.rem(me + 4 - step, 4)
        all_ref[pl.ds(pl.multiple_of(source * body, body), body), :] = ref[:body, :]
    small = lambda ref: ref[body:, :].astype(F32)
    summed = ((small(own_ref) + small(two_ref)) + (small(one_ref) + small(three_ref))) * factor
    bias_ref[...] = summed[:4, :]
    in_gain_ref[...] = summed[4:8, :]
    out_gain_ref[...] = summed[8:12, :]


def unpack_kernel(factor, *refs):
    uvqk_ref, out_ref = refs[8:]
    part = refs[0].shape[0] // 20
    width = uvqk_ref.shape[1] // 4
    block = width // 4
    batch = lax.axis_index("batch")
    core = lax.rem(batch, 2)
    y = batch // (lax.axis_size("batch") // 4)
    for side in range(2):
        at_core = core if side == 0 else 1 - core
        for number, step in enumerate((0, 1, 3, 2)):
            ref = refs[side * 4 + number]
            from_y = lax.rem(y + 4 - step, 4)
            place = pl.ds(pl.multiple_of((at_core * 4 + from_y) * part, part), part)
            for s in range(4):
                for b in range(5):
                    start = (s * 5 + b) * part
                    values = ref[start : start + part, :].astype(F32) * factor
                    if b < 4:
                        uvqk_ref[
                            place, s * width + b * block : s * width + (b + 1) * block
                        ] = values
                    else:
                        out_ref[place, s * block : (s + 1) * block] = values


PARAMS = pltpu.CompilerParams(vmem_limit_bytes=VMEM_LIMIT)


def shards(
    history,
    out_cotangent,
    lengths,
    bucket_of,
    position_bias,
    norm_gain,
    uvqk_weight,
    out_gain,
    out_weight,
):
    rows, width = history.shape[1:]
    heads, buckets = position_bias.shape
    seq_size = lax.axis_size("seq")
    batch_size = lax.axis_size("batch")
    total = rows * seq_size
    z_size = batch_size // 8
    factor = 1.0 / math.sqrt(batch_size * total)

    def along_x(values, step):
        return lax.ppermute(values, "seq", [(i, (i + step) % seq_size) for i in range(seq_size)])

    def along_batch(values, move):
        pairs = []
        for b in range(batch_size):
            y, z, c = b // (2 * z_size), (b // 2) % z_size, b % 2
            y, z, c = move(y, z, c)
            pairs.append((b, (y * z_size + z) * 2 + c))
        return lax.ppermute(values, "batch", pairs)

    def along_y(values, step):
        return along_batch(values, lambda y, z, c: ((y + step) % 4, z, c))

    def along_z(values, step):
        return along_batch(values, lambda y, z, c: (y, (z + step) % z_size, c))

    packed = jnp.concatenate([history[0], out_cotangent[0]], axis=1)
    pieces = [along_x(packed, step) for step in (1, 3, 2)]

    half = total // 2
    body = 5 * half
    shape = jax.ShapeDtypeStruct
    vmem = pl.BlockSpec(memory_space=pltpu.VMEM)
    smem = pl.BlockSpec(memory_space=pltpu.SMEM)
    output, grad_input, send, keep = pl.pallas_call(
        functools.partial(layer_kernel, seq_size),
        out_shape=[
            shape((rows, width), BF),
            shape((rows, width), BF),
            shape((body + 16, buckets), BF),
            shape((body + 16, buckets), F32),
        ],
        in_specs=[smem] + [vmem] * (seq_size + 7),
        out_specs=[vmem] * 4,
        scratch_shapes=[
            pltpu.VMEM((total, width), BF),
            pltpu.VMEM((total, width), BF),
            pltpu.VMEM((total, width), BF),
            pltpu.VMEM((total, width), F32),
            pltpu.VMEM((4, total, width), F32),
            pltpu.VMEM((3, total, width), BF),
            pltpu.VMEM((heads, rows, total), F32),
            pltpu.VMEM((total, width), BF),
            pltpu.VMEM((heads, total, total), BF),
            pltpu.VMEM((heads, total, total), BF),
            pltpu.VMEM((heads, rows, total), F32),
            pltpu.VMEM((total, width), BF),
            pltpu.VMEM((4, total, width), BF),
            pltpu.VMEM((heads, rows, total), F32),
        ],
        compiler_params=PARAMS,
        name="layer",
    )(
        lengths,
        history[0],
        out_cotangent[0],
        *pieces,
        bucket_of.reshape(1, total),
        position_bias,
        norm_gain.reshape(1, width),
        uvqk_weight,
        out_gain.reshape(1, width),
        out_weight,
    )

    got = along_batch(send, lambda y, z, c: (y, z, 1 - c))
    part = half // 4
    chunk = (5 * part + 16, buckets)
    own, *parts = pl.pallas_call(
        after_core_kernel,
        out_shape=[shape(chunk, F32)] + [shape(chunk, BF)] * 3,
        compiler_params=PARAMS,
        name="after_core",
    )(keep, got)
    parts = [along_y(values, step) for values, step in zip(parts, (1, 3, 2))]
    summed = pl.pallas_call(
        after_y_kernel, out_shape=shape(chunk, BF), compiler_params=PARAMS, name="after_y"
    )(own, *parts)
    other = along_batch(summed, lambda y, z, c: (y, z ^ 1, c))
    summed = pl.pallas_call(
        pair_sum_kernel, out_shape=shape(chunk, BF), compiler_params=PARAMS, name="pair_sum"
    )(summed, other)
    ring = [along_z(summed, step) for step in (2, 6, 4)]
    summed = pl.pallas_call(
        ring_sum_kernel, out_shape=shape(chunk, BF), compiler_params=PARAMS, name="ring_sum"
    )(summed, *ring)
    blocks = [along_x(summed, step) for step in (1, 3, 2)]
    gathered, grad_bias, grad_in_gain, grad_out_gain = pl.pallas_call(
        functools.partial(after_x_kernel, factor),
        out_shape=[shape((20 * part, buckets), BF)] + [shape((4, buckets), F32)] * 3,
        compiler_params=PARAMS,
        name="after_x",
    )(summed, *blocks)
    columns = [gathered] + [along_y(gathered, step) for step in (1, 3, 2)]
    others = [along_batch(values, lambda y, z, c: (y, z, 1 - c)) for values in columns]
    grad_uvqk, grad_out_weight = pl.pallas_call(
        functools.partial(unpack_kernel, factor),
        out_shape=[shape((width, 4 * width), F32), shape((width, width), F32)],
        compiler_params=PARAMS,
        name="unpack",
    )(*columns, *others)
    return (
        output[None],
        grad_input[None],
        grad_uvqk,
        grad_out_weight,
        grad_bias,
        grad_in_gain.reshape(width),
        grad_out_gain.reshape(width),
    )


def solution(mesh):
    return jax.shard_map(
        shards,
        mesh=mesh,
        in_specs=(
            P("batch", "seq", None),
            P("batch", "seq", None),
            P("batch"),
            P(),
            P(),
            P(),
            P(),
            P(),
            P(),
        ),
        out_specs=(P("batch", "seq", None), P("batch", "seq", None), P(), P(), P(), P(), P()),
        check_vma=False,
    )
```

```python
import functools
import math

import jax
import jax.numpy as jnp
from jax import lax
from jax.experimental import pallas as pl
from jax.experimental.pallas import tpu as pltpu
from jax.sharding import PartitionSpec as P

NORM_EPS = 1e-05
BF = jnp.bfloat16
F32 = jnp.float32
LARGE = 30 * 1024 * 1024
SMALL = 12 * 1024 * 1024
STEPS = (0, 1, 3, 2)
UNPACK_FLOPS = 10**10
HIDDEN = -1e9


def normalize(values):
    centered = values - jnp.mean(values, axis=-1, keepdims=True)
    inv_scale = lax.rsqrt(jnp.mean(centered * centered, axis=-1, keepdims=True) + NORM_EPS)
    return (centered * inv_scale, inv_scale)


def norm_backward(grad_normed, normed, inv_scale):
    return inv_scale * (
        grad_normed
        - jnp.mean(grad_normed, axis=-1, keepdims=True)
        - normed * jnp.mean(grad_normed * normed, axis=-1, keepdims=True)
    )


def sigmoid(values):
    return 0.5 * jnp.tanh(0.5 * values) + 0.5


def dot_nn(left, right):
    return lax.dot_general(left, right, (((1,), (0,)), ((), ())), preferred_element_type=F32)


def dot_nt(left, right):
    return lax.dot_general(left, right, (((1,), (1,)), ((), ())), preferred_element_type=F32)


def dot_tn(left, right):
    return lax.dot_general(left, right, (((0,), (0,)), ((), ())), preferred_element_type=F32)


def three_parts(values):
    high = values.astype(BF)
    rest = values - high.astype(F32)
    middle = rest.astype(BF)
    low = (rest - middle.astype(F32)).astype(BF)
    return high, middle, low


def as_rows(row, parts):
    width = row.shape[1] // parts
    return jnp.concatenate([row[:, p * width : (p + 1) * width] for p in range(parts)], axis=0)


def prepare_kernel(
    bucket_hbm,
    bias_hbm,
    history_hbm,
    cotangent_hbm,
    in_gain_hbm,
    out_gain_hbm,
    uvqk_hbm,
    out_w_hbm,
    own_ref,
    own_cot_ref,
    in_gain_ref,
    out_gain_ref,
    uvqk_ref,
    out_w_ref,
    tile_ref,
    onehot_ref,
    bucket_ref,
    bias_ref,
    sems,
):
    copies = [
        pltpu.make_async_copy(source, target, sems.at[n])
        for n, (source, target) in enumerate(
            (
                (bucket_hbm, bucket_ref),
                (bias_hbm, bias_ref),
                (history_hbm, own_ref),
                (in_gain_hbm, in_gain_ref),
                (uvqk_hbm, uvqk_ref),
                (cotangent_hbm, own_cot_ref),
                (out_gain_hbm, out_gain_ref),
                (out_w_hbm, out_w_ref),
            )
        )
    ]
    for copy in copies:
        copy.start()
    heads, buckets = bias_ref.shape
    rows = own_ref.shape[0]
    total = bucket_ref.shape[1]
    copies[0].wait()
    copies[1].wait()

    span = total + rows
    offset = total - rows
    turned = offset - lax.broadcasted_iota(jnp.int32, (total, span), 1)
    turned = jnp.where(turned < 0, turned + span, turned)
    pick = (lax.broadcasted_iota(jnp.int32, (total, span), 0) == turned).astype(F32).astype(BF)
    bucket_rows = jnp.broadcast_to(bucket_ref[...].astype(F32), (8, total)).astype(BF)
    bucket_row = dot_nn(bucket_rows, pick)[:1, :]
    column = offset - lax.broadcasted_iota(jnp.int32, (1, span), 1)
    seen = jnp.where(column < 0, column + span, column) < total
    bucket_row = jnp.where(seen, bucket_row, -1.0)
    onehot = (
        lax.broadcasted_iota(jnp.int32, (buckets, span), 0).astype(F32)
        == jnp.broadcast_to(bucket_row, (buckets, span))
    ).astype(F32).astype(BF)
    onehot_ref[...] = onehot
    bias_rows = jnp.concatenate([bias_ref[...], jnp.zeros((8 - heads, buckets), F32)], axis=0)
    by_distance = sum(dot_nn(part, onehot) for part in three_parts(bias_rows))
    by_distance = jnp.where(seen, by_distance, HIDDEN)
    for h in range(heads):
        skewed = pltpu.roll(
            jnp.broadcast_to(by_distance[h : h + 1, :], (rows, span)), 0, 1, stride=1, stride_axis=0
        )
        tile_ref[h] = skewed[:, :total]
    for copy in copies[2:]:
        copy.wait()


def place_pieces(refs, target, size):
    me = lax.axis_index("seq")
    for step, ref in zip(STEPS, refs):
        source = lax.rem(me + size - step, size)
        rows = ref.shape[0]
        target[pl.ds(pl.multiple_of(source * rows, rows), rows), :] = ref[...]


def forward_kernel(size, *refs):
    pieces = refs[:size]
    (
        tile_ref,
        in_gain_ref,
        uvqk_ref,
        scaled_ref,
        gate_ref,
        slope_ref,
        vqk_ref,
        weights_ref,
        score_slope_ref,
        mixed_ref,
        hist_s,
    ) = refs[size:]
    rows, width = pieces[0].shape
    total = rows * size
    heads = tile_ref.shape[0]
    head_dim = width // heads
    scale = 1.0 / math.sqrt(head_dim)
    in_gain = in_gain_ref[...]
    place_pieces(pieces, hist_s, size)
    for i in range(size):
        here = slice(i * rows, (i + 1) * rows)
        ends = (i + 1) * rows
        first = total - ends
        normed, _ = normalize(hist_s[here, :].astype(F32))
        scaled = (normed * in_gain).astype(BF)
        scaled_ref[here, :] = scaled
        for part in range(4):
            projected = dot_nn(scaled, uvqk_ref[:, part * width : (part + 1) * width])
            sig = sigmoid(projected)
            activated = projected * sig
            slope_ref[part, here, :] = sig + activated * (1.0 - sig)
            if part == 0:
                gate_ref[here, :] = activated
            else:
                vqk_ref[part - 1, here, :] = activated.astype(BF)
        for h in range(heads):
            lanes = slice(h * head_dim, (h + 1) * head_dim)
            scores = dot_nt(vqk_ref[1, here, lanes], vqk_ref[2, :ends, lanes]) * scale
            scores = scores + tile_ref[h, :, first:]
            sig = sigmoid(scores)
            weights = scores * sig
            score_slope_ref[h, here, :ends] = sig + weights * (1.0 - sig)
            weights_low = weights.astype(BF)
            weights_ref[h, here, :ends] = weights_low
            mixed_ref[here, lanes] = dot_nn(weights_low, vqk_ref[0, :ends, lanes])


def backward_kernel(size, length_ref, *refs):
    pieces = refs[:size]
    (
        out_gain_ref,
        out_w_ref,
        scaled_ref,
        gate_ref,
        slope_ref,
        vqk_ref,
        weights_ref,
        score_slope_ref,
        mixed_ref,
        send_ref,
        keep_ref,
        own_gated_ref,
        own_grad_ref,
        diag_ref,
        gain_ref,
        cot_s,
        gated_s,
        grads_s,
        grad_mixed_s,
        proj_grad_s,
    ) = refs[size:]
    rows, width = pieces[0].shape
    total = rows * size
    heads = weights_ref.shape[0]
    head_dim = width // heads
    scale = 1.0 / math.sqrt(head_dim)
    me = lax.axis_index("seq")
    core = lax.rem(lax.axis_index("batch"), 2)
    length = length_ref[0]
    out_gain = out_gain_ref[...]
    place_pieces(pieces, cot_s, size)
    grad_out_gain = jnp.zeros((1, width), F32)
    for h in range(heads):
        diag_ref[h] = jnp.zeros((rows, total), F32)
    for i in range(size):
        here = slice(i * rows, (i + 1) * rows)
        ends = (i + 1) * rows
        first = total - ends
        valid = (lax.broadcasted_iota(jnp.int32, (rows, 1), 0) + i * rows) < length
        mixed = jnp.where(valid, mixed_ref[here, :], 0.0)
        mixed_normed, inv_mixed = normalize(mixed)
        gating = gate_ref[here, :]
        gated_s[here, :] = (mixed_normed * out_gain * gating).astype(BF)
        grad_gated = dot_nt(cot_s[here, :], out_w_ref[...])
        times_normed = grad_gated * mixed_normed
        grad_out_gain = grad_out_gain + jnp.sum(times_normed * gating, axis=0, keepdims=True)
        proj_grad_s[0, here, :] = (times_normed * out_gain * slope_ref[0, here, :]).astype(BF)
        grad_mixed = norm_backward(grad_gated * out_gain * gating, mixed_normed, inv_mixed)
        grad_mixed_low = jnp.where(valid, grad_mixed, 0.0).astype(BF)
        grad_mixed_s[here, :] = grad_mixed_low
        for h in range(heads):
            lanes = slice(h * head_dim, (h + 1) * head_dim)
            grad_weights = dot_nt(grad_mixed_low[:, lanes], vqk_ref[0, :ends, lanes])
            grad_scores = grad_weights * score_slope_ref[h, here, :ends]
            diag_ref[h, :, first:] += grad_scores
            grad_scores_low = grad_scores.astype(BF)
            grads_s[h, here, :ends] = grad_scores_low
            grad_query = dot_nn(grad_scores_low, vqk_ref[2, :ends, lanes]) * scale
            proj_grad_s[2, here, lanes] = (grad_query * slope_ref[2, here, lanes]).astype(BF)
    gain_ref[...] = grad_out_gain

    for j in range(size):
        here = slice(j * rows, (j + 1) * rows)
        later = slice(j * rows, total)
        for h in range(heads):
            lanes = slice(h * head_dim, (h + 1) * head_dim)
            grad_key = dot_tn(grads_s[h, later, here], vqk_ref[1, later, lanes]) * scale
            proj_grad_s[3, here, lanes] = (grad_key * slope_ref[3, here, lanes]).astype(BF)
            grad_value = dot_tn(weights_ref[h, later, here], grad_mixed_s[later, lanes])
            proj_grad_s[1, here, lanes] = (grad_value * slope_ref[1, here, lanes]).astype(BF)

    half = total // 2
    block = width // 4
    own_block = proj_grad_s[me]
    cot_block = cot_s[:, pl.ds(pl.multiple_of(me * block, block), block)]
    for ref, side in ((send_ref, 1 - core), (keep_ref, core)):
        lanes = pl.ds(pl.multiple_of(side * half, half), half)
        uvqk_term = dot_tn(scaled_ref[:, lanes], own_block)
        for b in range(4):
            ref[b * half : (b + 1) * half, :] = uvqk_term[:, b * block : (b + 1) * block].astype(
                ref.dtype
            )
        out_term = dot_tn(gated_s[:, lanes], cot_block)
        ref[4 * half : 5 * half, :] = out_term.astype(ref.dtype)
    own_rows = pl.ds(pl.multiple_of(me * rows, rows), rows)
    own_gated_ref[...] = gated_s[own_rows, :]
    for part in range(4):
        own_grad_ref[part] = proj_grad_s[part, own_rows, :]


def rows_kernel(
    own_ref,
    own_cot_ref,
    in_gain_ref,
    uvqk_ref,
    out_w_ref,
    own_gated_ref,
    own_grad_ref,
    diag_ref,
    gain_ref,
    onehot_ref,
    output_ref,
    grad_input_ref,
    small_ref,
):
    rows, width = own_ref.shape
    heads, _, total = diag_ref.shape
    buckets, span = onehot_ref.shape
    me = lax.axis_index("seq")
    in_gain = in_gain_ref[...]
    wide = own_ref[...].astype(F32)
    normed, inv_in = normalize(wide)
    grad_scaled = jnp.zeros((rows, width), F32)
    for part in range(4):
        grad_scaled = grad_scaled + dot_nt(
            own_grad_ref[part], uvqk_ref[:, part * width : (part + 1) * width]
        )
    grad_in_gain = jnp.sum(grad_scaled * normed, axis=0, keepdims=True)
    grad_input = own_cot_ref[...].astype(F32) + norm_backward(grad_scaled * in_gain, normed, inv_in)
    grad_input_ref[...] = grad_input.astype(BF)
    output_ref[...] = (wide + dot_nn(own_gated_ref[...], out_w_ref[...])).astype(BF)

    onehot = onehot_ref[...]
    bias_sums = []
    for h in range(heads):
        folded = jnp.concatenate([diag_ref[h], jnp.zeros((rows, span - total), F32)], axis=1)
        count = rows // 2
        while count >= 8:
            folded = folded[:count, :] + pltpu.roll(folded[count:, :], span - count, 1)
            count //= 2
        while count >= 1:
            folded = folded + pltpu.roll(pltpu.roll(folded, 8 - count, 0), span - count, 1)
            count //= 2
        bias_sums.append(folded[:1, :])
    bias_sums = jnp.concatenate(bias_sums + [jnp.zeros((8 - heads, span), F32)], axis=0)
    grad_bias = sum(dot_nt(part, onehot) for part in three_parts(bias_sums))[:heads, :]
    small = jnp.concatenate(
        [
            grad_bias,
            as_rows(grad_in_gain, 4),
            as_rows(gain_ref[...], 4),
            jnp.zeros((4, buckets), F32),
        ],
        axis=0,
    )
    row = lax.broadcasted_iota(jnp.int32, small.shape, 0)
    mine = (row == me) | ((row >= 4) & (row < 8)) | (row == 8 + me)
    small_ref[...] = jnp.where(mine, small, 0.0)


def after_core_kernel(keep_ref, got_ref, small_ref, own_ref, *others):
    half = keep_ref.shape[0] // 5
    part = half // 4
    y = lax.axis_index("batch") // (lax.axis_size("batch") // 4)
    for ref, step in zip((own_ref,) + others, STEPS):
        there = lax.rem(y + step, 4)
        for b in range(5):
            place = pl.ds(pl.multiple_of(b * half + there * part, part), part)
            ref[b * part : (b + 1) * part, :] = (
                keep_ref[place, :] + got_ref[place, :].astype(F32)
            ).astype(ref.dtype)
        ref[5 * part :, :] = small_ref[...].astype(ref.dtype)


def after_y_kernel(own_ref, one_ref, three_ref, two_ref, sum_ref):
    body = own_ref.shape[0] - 16
    got = lambda ref, place: ref[place, :].astype(F32)
    for place, own in (
        (slice(0, body), own_ref[:body, :]),
        (slice(body, None), own_ref[body:, :].astype(BF).astype(F32)),
    ):
        sum_ref[place, :] = (
            (own + got(two_ref, place)) + (got(one_ref, place) + got(three_ref, place))
        ).astype(BF)


def pair_sum_kernel(left_ref, right_ref, sum_ref):
    sum_ref[...] = (left_ref[...].astype(F32) + right_ref[...].astype(F32)).astype(BF)


def ring_sum_kernel(own_ref, two_ref, six_ref, four_ref, sum_ref):
    sum_ref[...] = (
        (own_ref[...].astype(F32) + four_ref[...].astype(F32))
        + (two_ref[...].astype(F32) + six_ref[...].astype(F32))
    ).astype(BF)


def join_kernel(*refs):
    joined = refs[-1]
    size = refs[0].shape[0]
    for n, ref in enumerate(refs[:-1]):
        joined[n * size : (n + 1) * size, :] = ref[...]


def unpack(factor, sources, kept, *refs):
    blocks = refs[: len(sources)]
    uvqk_hbm, out_hbm, wide_s, narrow_s, sems = refs[len(sources) + kept :]
    size = blocks[0].shape[0] // 4
    part = (size - 16) // 5
    width = uvqk_hbm.shape[1] // 4
    block = width // 4
    batch = lax.axis_index("batch")
    core = lax.rem(batch, 2)
    x = lax.axis_index("seq")
    y = batch // (lax.axis_size("batch") // 4)
    copies = []
    for n, (ref, (other, second)) in enumerate(zip(blocks, sources)):
        from_core = 1 - core if other else core
        x_first = from_core == 0
        for m, first in enumerate(STEPS):
            slot = n * 4 + m
            from_x = lax.rem(x + 4 - jnp.where(x_first, first, second), 4)
            from_y = lax.rem(y + 4 - jnp.where(x_first, second, first), 4)
            start = m * size
            for b in range(4):
                wide_s[slot, :, b * block : (b + 1) * block] = (
                    ref[start + b * part : start + (b + 1) * part, :].astype(F32) * factor
                )
            narrow_s[slot] = ref[start + 4 * part : start + 5 * part, :].astype(F32) * factor
            place = pl.ds(pl.multiple_of((from_core * 4 + from_y) * part, part), part)
            for copy in (
                pltpu.make_async_copy(
                    wide_s.at[slot],
                    uvqk_hbm.at[place, pl.ds(pl.multiple_of(from_x * width, width), width)],
                    sems.at[slot, 0],
                ),
                pltpu.make_async_copy(
                    narrow_s.at[slot],
                    out_hbm.at[place, pl.ds(pl.multiple_of(from_x * block, block), block)],
                    sems.at[slot, 1],
                ),
            ):
                copy.start()
                copies.append(copy)
    return copies


def unpack_kernel(factor, sources, kept, *refs):
    for copy in unpack(factor, sources, kept, *refs):
        copy.wait()


def last_kernel(factor, sources, kept, *refs):
    blocks = refs[:8]
    unpacked = refs[8 - len(sources) : 8 + kept]
    uvqk_hbm, out_hbm, bias_ref, in_gain_ref, out_gain_ref = refs[8 + kept : 13 + kept]
    copies = unpack(factor, sources, kept, *unpacked, uvqk_hbm, out_hbm, *refs[13 + kept :])
    size = blocks[0].shape[0] // 4
    core = lax.rem(lax.axis_index("batch"), 2)

    def piece(ref, first):
        place = (first + 1) * size
        return ref[place - 16 : place, :].astype(F32)

    def over_x(own, x_first):
        by_first = [piece(own[0], n) for n in range(4)]
        by_second = [piece(own[n], 0) for n in range(4)]
        zero, one, three, two = [
            jnp.where(x_first, left, right) for left, right in zip(by_first, by_second)
        ]
        return (zero + two) + (one + three)

    summed = (over_x(blocks[:4], core == 0) + over_x(blocks[4:], core == 1)) * factor
    bias_ref[...] = summed[:4, :]
    in_gain_ref[...] = summed[4:8, :]
    out_gain_ref[...] = summed[8:12, :]
    for copy in copies:
        copy.wait()


def params(limit):
    return pltpu.CompilerParams(vmem_limit_bytes=limit)


def cost(flops, bytes_accessed):
    return pl.CostEstimate(flops=flops, bytes_accessed=bytes_accessed, transcendentals=0)


def shards(
    history,
    out_cotangent,
    lengths,
    bucket_of,
    position_bias,
    norm_gain,
    uvqk_weight,
    out_gain,
    out_weight,
):
    rows, width = history.shape[1:]
    heads, buckets = position_bias.shape
    seq_size = lax.axis_size("seq")
    batch_size = lax.axis_size("batch")
    total = rows * seq_size
    span = total + rows
    z_size = batch_size // 8
    factor = 1.0 / math.sqrt(batch_size * total)

    def along_x(values, step):
        return lax.ppermute(values, "seq", [(i, (i + step) % seq_size) for i in range(seq_size)])

    def place_of(b):
        return b // (2 * z_size), (b // 2) % z_size, b % 2

    def along_batch(values, move):
        pairs = []
        for b in range(batch_size):
            y, z, c = move(*place_of(b))
            pairs.append((b, (y * z_size + z) * 2 + c))
        return lax.ppermute(values, "batch", pairs)

    def along_y(values, step):
        return along_batch(values, lambda y, z, c: ((y + step) % 4, z, c))

    def along_z(values, step):
        return along_batch(values, lambda y, z, c: (y, (z + step) % z_size, c))

    def across(values):
        return along_batch(values, lambda y, z, c: (y, z, 1 - c))

    def along_either(values, step, x_core):
        pairs = []
        for x in range(seq_size):
            for b in range(batch_size):
                y, z, c = place_of(b)
                to_x = (x + step) % 4 if c == x_core else x
                to_y = y if c == x_core else (y + step) % 4
                pairs.append(
                    (x * batch_size + b, to_x * batch_size + (to_y * z_size + z) * 2 + c)
                )
        return lax.ppermute(values, ("seq", "batch"), pairs)

    shape = jax.ShapeDtypeStruct
    vmem = pl.BlockSpec(memory_space=pltpu.VMEM)
    smem = pl.BlockSpec(memory_space=pltpu.SMEM)
    hbm = pl.BlockSpec(memory_space=pltpu.HBM)
    own_history = history[0]
    own_cotangent = out_cotangent[0]
    pieces = [along_x(own_history, step) for step in STEPS[1:]]
    cot_pieces = [along_x(own_cotangent, step) for step in STEPS[1:]]
    own, own_cot, in_gain, gain, uvqk, out_w, tile, onehot = pl.pallas_call(
        prepare_kernel,
        out_shape=[
            shape((rows, width), BF),
            shape((rows, width), BF),
            shape((1, width), F32),
            shape((1, width), F32),
            shape(uvqk_weight.shape, BF),
            shape(out_weight.shape, BF),
            shape((heads, rows, total), F32),
            shape((buckets, span), BF),
        ],
        in_specs=[hbm] * 8,
        out_specs=[vmem] * 8,
        scratch_shapes=[
            pltpu.VMEM((1, total), jnp.int32),
            pltpu.VMEM((heads, buckets), F32),
            pltpu.SemaphoreType.DMA((8,)),
        ],
        compiler_params=params(SMALL),
        cost_estimate=cost(10**9, 3 * 10**6),
        name="prepare",
    )(
        *[
            pltpu.with_memory_space_constraint(values, pltpu.HBM)
            for values in (
                bucket_of.reshape(1, total),
                position_bias,
                own_history,
                own_cotangent,
                norm_gain.reshape(1, width),
                out_gain.reshape(1, width),
                uvqk_weight,
                out_weight,
            )
        ]
    )
    scaled, gate, slope, vqk, weights, score_slope, mixed = pl.pallas_call(
        functools.partial(forward_kernel, seq_size),
        out_shape=[
            shape((total, width), BF),
            shape((total, width), F32),
            shape((4, total, width), F32),
            shape((3, total, width), BF),
            shape((heads, total, total), BF),
            shape((heads, total, total), F32),
            shape((total, width), F32),
        ],
        scratch_shapes=[pltpu.VMEM((total, width), BF)],
        compiler_params=params(LARGE),
        cost_estimate=cost(4 * 10**9, 10**7),
        name="forward",
    )(own, *pieces, tile, in_gain, uvqk)
    half = total // 2
    body = 5 * half
    send, keep, own_gated, own_grad, diag, gain_term = pl.pallas_call(
        functools.partial(backward_kernel, seq_size),
        out_shape=[
            shape((body, buckets), BF),
            shape((body, buckets), F32),
            shape((rows, width), BF),
            shape((4, rows, width), BF),
            shape((heads, rows, total), F32),
            shape((1, width), F32),
        ],
        in_specs=[smem] + [vmem] * 13,
        out_specs=[vmem] * 6,
        scratch_shapes=[
            pltpu.VMEM((total, width), BF),
            pltpu.VMEM((total, width), BF),
            pltpu.VMEM((heads, total, total), BF),
            pltpu.VMEM((total, width), BF),
            pltpu.VMEM((4, total, width), BF),
        ],
        compiler_params=params(LARGE),
        cost_estimate=cost(4 * 10**9, 10**7),
        name="backward",
    )(
        lengths,
        own_cot,
        *cot_pieces,
        gain,
        out_w,
        scaled,
        gate,
        slope,
        vqk,
        weights,
        score_slope,
        mixed,
    )

    got = across(send)
    output, grad_input, small = pl.pallas_call(
        rows_kernel,
        out_shape=[
            shape((rows, width), BF),
            shape((rows, width), BF),
            shape((16, buckets), F32),
        ],
        compiler_params=params(SMALL),
        cost_estimate=cost(10**9, 3 * 10**6),
        name="rows",
    )(own, own_cot, in_gain, uvqk, out_w, own_gated, own_grad, diag, gain_term, onehot)

    part = half // 4
    size = 5 * part + 16
    chunk = (size, buckets)
    mine, *parts = pl.pallas_call(
        after_core_kernel,
        out_shape=[shape(chunk, F32)] + [shape(chunk, BF)] * 3,
        compiler_params=params(SMALL),
        name="after_core",
    )(keep, got, small)
    parts = [along_y(values, step) for values, step in zip(parts, STEPS[1:])]
    summed = pl.pallas_call(
        after_y_kernel, out_shape=shape(chunk, BF), compiler_params=params(SMALL), name="after_y"
    )(mine, *parts)
    other = along_batch(summed, lambda y, z, c: (y, z ^ 1, c))
    summed = pl.pallas_call(
        pair_sum_kernel, out_shape=shape(chunk, BF), compiler_params=params(SMALL), name="pair_sum"
    )(summed, other)
    ring = [along_z(summed, step) for step in (2, 6, 4)]
    summed = pl.pallas_call(
        ring_sum_kernel, out_shape=shape(chunk, BF), compiler_params=params(SMALL), name="ring_sum"
    )(summed, *ring)

    blocks = [along_either(summed, step, 0) for step in STEPS[1:]]
    joined = pl.pallas_call(
        join_kernel,
        out_shape=shape((4 * size, buckets), BF),
        compiler_params=params(SMALL),
        name="join",
    )(summed, *blocks)
    columns, others = {0: joined}, {}
    def unpack_call(sources, kept, last=False):
        blocks = [(others if other else columns)[step] for other, step in sources]
        slots = 4 * len(blocks)
        outs = [shape((width, 4 * width), F32), shape((width, width), F32)]
        if last:
            blocks = [columns[step] for step in STEPS] + [others[step] for step in STEPS]
        count = len(blocks)
        return pl.pallas_call(
            functools.partial(last_kernel if last else unpack_kernel, factor, sources, len(kept)),
            out_shape=outs + [shape((4, buckets), F32)] * (3 if last else 0),
            in_specs=[vmem] * count + [hbm] * len(kept),
            out_specs=[hbm] * 2 + [vmem] * (3 if last else 0),
            input_output_aliases={count + n: n for n in range(len(kept))},
            scratch_shapes=[
                pltpu.VMEM((slots, part, width), F32),
                pltpu.VMEM((slots, part, buckets), F32),
                pltpu.SemaphoreType.DMA((slots, 2)),
            ],
            compiler_params=params(SMALL),
            cost_estimate=cost(UNPACK_FLOPS, 10**6 * slots // 4),
            name="unpack",
        )(*blocks, *kept)

    moved = {step: along_either(joined, step, 1) for step in STEPS[1:]}
    kept = unpack_call(((False, 0),), ())
    again, kept = lax.optimization_barrier((joined, kept))
    others[0] = across(again)
    for step in STEPS[1:]:
        columns[step], kept = lax.optimization_barrier((moved[step], kept))
        others[step] = across(columns[step])
    kept = unpack_call(((True, 0), (False, 1), (False, 3), (False, 2)), kept)
    grad_uvqk, grad_out_weight, grad_bias, grad_in_gain, grad_out_gain = unpack_call(
        ((True, 1), (True, 3), (True, 2)), kept, last=True
    )
    return (
        output[None],
        grad_input[None],
        grad_uvqk,
        grad_out_weight,
        grad_bias,
        grad_in_gain.reshape(width),
        grad_out_gain.reshape(width),
    )


def solution(mesh):
    return jax.shard_map(
        shards,
        mesh=mesh,
        in_specs=(
            P("batch", "seq", None),
            P("batch", "seq", None),
            P("batch"),
            P(),
            P(),
            P(),
            P(),
            P(),
            P(),
        ),
        out_specs=(P("batch", "seq", None), P("batch", "seq", None), P(), P(), P(), P(), P()),
        check_vma=False,
    )
```

```python
import functools
import math

import jax
import jax.numpy as jnp
from jax import lax
from jax.experimental import pallas as pl
from jax.experimental.pallas import tpu as pltpu
from jax.sharding import PartitionSpec as P

NORM_EPS = 1e-05
BF = jnp.bfloat16
F32 = jnp.float32
LARGE = 30 * 1024 * 1024
SMALL = 12 * 1024 * 1024
STEPS = (0, 1, 3, 2)
UNPACK_FLOPS = 10**10
HIDDEN = -1e9


def normalize(values):
    centered = values - jnp.mean(values, axis=-1, keepdims=True)
    inv_scale = lax.rsqrt(jnp.mean(centered * centered, axis=-1, keepdims=True) + NORM_EPS)
    return (centered * inv_scale, inv_scale)


def norm_backward(grad_normed, normed, inv_scale):
    return inv_scale * (
        grad_normed
        - jnp.mean(grad_normed, axis=-1, keepdims=True)
        - normed * jnp.mean(grad_normed * normed, axis=-1, keepdims=True)
    )


def sigmoid(values):
    return 0.5 * jnp.tanh(0.5 * values) + 0.5


def dot_nn(left, right):
    return lax.dot_general(left, right, (((1,), (0,)), ((), ())), preferred_element_type=F32)


def dot_nt(left, right):
    return lax.dot_general(left, right, (((1,), (1,)), ((), ())), preferred_element_type=F32)


def dot_tn(left, right):
    return lax.dot_general(left, right, (((0,), (0,)), ((), ())), preferred_element_type=F32)


def three_parts(values):
    high = values.astype(BF)
    rest = values - high.astype(F32)
    middle = rest.astype(BF)
    low = (rest - middle.astype(F32)).astype(BF)
    return high, middle, low


def as_rows(row, parts):
    width = row.shape[1] // parts
    return jnp.concatenate([row[:, p * width : (p + 1) * width] for p in range(parts)], axis=0)


def prepare_kernel(
    bucket_hbm,
    bias_hbm,
    history_hbm,
    cotangent_hbm,
    in_gain_hbm,
    out_gain_hbm,
    uvqk_hbm,
    out_w_hbm,
    own_ref,
    own_cot_ref,
    in_gain_ref,
    out_gain_ref,
    uvqk_ref,
    out_w_ref,
    tile_ref,
    onehot_ref,
    bucket_ref,
    bias_ref,
    sems,
):
    copies = [
        pltpu.make_async_copy(source, target, sems.at[n])
        for n, (source, target) in enumerate(
            (
                (bucket_hbm, bucket_ref),
                (bias_hbm, bias_ref),
                (history_hbm, own_ref),
                (in_gain_hbm, in_gain_ref),
                (uvqk_hbm, uvqk_ref),
                (cotangent_hbm, own_cot_ref),
                (out_gain_hbm, out_gain_ref),
                (out_w_hbm, out_w_ref),
            )
        )
    ]
    for copy in copies:
        copy.start()
    heads, buckets = bias_ref.shape
    rows = own_ref.shape[0]
    total = bucket_ref.shape[1]
    copies[0].wait()
    copies[1].wait()

    span = total + rows
    offset = total - rows
    turned = offset - lax.broadcasted_iota(jnp.int32, (total, span), 1)
    turned = jnp.where(turned < 0, turned + span, turned)
    pick = (lax.broadcasted_iota(jnp.int32, (total, span), 0) == turned).astype(F32).astype(BF)
    bucket_rows = jnp.broadcast_to(bucket_ref[...].astype(F32), (8, total)).astype(BF)
    bucket_row = dot_nn(bucket_rows, pick)[:1, :]
    column = offset - lax.broadcasted_iota(jnp.int32, (1, span), 1)
    seen = jnp.where(column < 0, column + span, column) < total
    bucket_row = jnp.where(seen, bucket_row, -1.0)
    onehot = (
        lax.broadcasted_iota(jnp.int32, (buckets, span), 0).astype(F32)
        == jnp.broadcast_to(bucket_row, (buckets, span))
    ).astype(F32).astype(BF)
    onehot_ref[...] = onehot
    bias_rows = jnp.concatenate([bias_ref[...], jnp.zeros((8 - heads, buckets), F32)], axis=0)
    by_distance = sum(dot_nn(part, onehot) for part in three_parts(bias_rows))
    by_distance = jnp.where(seen, by_distance, HIDDEN)
    for h in range(heads):
        skewed = pltpu.roll(
            jnp.broadcast_to(by_distance[h : h + 1, :], (rows, span)), 0, 1, stride=1, stride_axis=0
        )
        tile_ref[h] = skewed[:, :total]
    for copy in copies[2:]:
        copy.wait()


def square_index():
    batch = lax.axis_index("batch")
    z_size = lax.axis_size("batch") // 8
    y = batch // (2 * z_size)
    z = lax.rem(batch // 2, z_size)
    bit = lambda place: lax.rem((place + 1) // 2, 2)
    return 2 * bit(y) + bit(z)


def place_pieces(refs, target, size):
    me = lax.axis_index("seq")
    for step, ref in zip(STEPS, refs):
        source = lax.rem(me + size - step, size)
        rows = ref.shape[0]
        target[pl.ds(pl.multiple_of(source * rows, rows), rows), :] = ref[...]


def forward_kernel(size, *refs):
    pieces = refs[:size]
    (
        tile_ref,
        in_gain_ref,
        uvqk_ref,
        scaled_ref,
        gate_ref,
        slope_ref,
        vqk_ref,
        weights_ref,
        score_slope_ref,
        mixed_ref,
        hist_s,
    ) = refs[size:]
    rows, width = pieces[0].shape
    total = rows * size
    heads = tile_ref.shape[0]
    head_dim = width // heads
    scale = 1.0 / math.sqrt(head_dim)
    in_gain = in_gain_ref[...]
    place_pieces(pieces, hist_s, size)
    for i in range(size):
        here = slice(i * rows, (i + 1) * rows)
        ends = (i + 1) * rows
        first = total - ends
        normed, _ = normalize(hist_s[here, :].astype(F32))
        scaled = (normed * in_gain).astype(BF)
        scaled_ref[here, :] = scaled
        for part in range(4):
            projected = dot_nn(scaled, uvqk_ref[:, part * width : (part + 1) * width])
            sig = sigmoid(projected)
            activated = projected * sig
            slope_ref[part, here, :] = sig + activated * (1.0 - sig)
            if part == 0:
                gate_ref[here, :] = activated
            else:
                vqk_ref[part - 1, here, :] = activated.astype(BF)
        for h in range(heads):
            lanes = slice(h * head_dim, (h + 1) * head_dim)
            scores = dot_nt(vqk_ref[1, here, lanes], vqk_ref[2, :ends, lanes]) * scale
            scores = scores + tile_ref[h, :, first:]
            sig = sigmoid(scores)
            weights = scores * sig
            score_slope_ref[h, here, :ends] = sig + weights * (1.0 - sig)
            weights_low = weights.astype(BF)
            weights_ref[h, here, :ends] = weights_low
            mixed_ref[here, lanes] = dot_nn(weights_low, vqk_ref[0, :ends, lanes])


def backward_kernel(size, length_ref, *refs):
    pieces = refs[:size]
    (
        out_gain_ref,
        out_w_ref,
        scaled_ref,
        gate_ref,
        slope_ref,
        vqk_ref,
        weights_ref,
        score_slope_ref,
        mixed_ref,
        send_ref,
        keep_ref,
        own_gated_ref,
        own_grad_ref,
        diag_ref,
        gain_ref,
        cot_s,
        gated_s,
        grads_s,
        grad_mixed_s,
        proj_grad_s,
    ) = refs[size:]
    rows, width = pieces[0].shape
    total = rows * size
    heads = weights_ref.shape[0]
    head_dim = width // heads
    scale = 1.0 / math.sqrt(head_dim)
    me = lax.axis_index("seq")
    core = lax.rem(lax.axis_index("batch"), 2)
    length = length_ref[0]
    out_gain = out_gain_ref[...]
    place_pieces(pieces, cot_s, size)
    grad_out_gain = jnp.zeros((1, width), F32)
    for h in range(heads):
        diag_ref[h] = jnp.zeros((rows, total), F32)
    for i in range(size):
        here = slice(i * rows, (i + 1) * rows)
        ends = (i + 1) * rows
        first = total - ends
        valid = (lax.broadcasted_iota(jnp.int32, (rows, 1), 0) + i * rows) < length
        mixed = jnp.where(valid, mixed_ref[here, :], 0.0)
        mixed_normed, inv_mixed = normalize(mixed)
        gating = gate_ref[here, :]
        gated_s[here, :] = (mixed_normed * out_gain * gating).astype(BF)
        grad_gated = dot_nt(cot_s[here, :], out_w_ref[...])
        times_normed = grad_gated * mixed_normed
        grad_out_gain = grad_out_gain + jnp.sum(times_normed * gating, axis=0, keepdims=True)
        proj_grad_s[0, here, :] = (times_normed * out_gain * slope_ref[0, here, :]).astype(BF)
        grad_mixed = norm_backward(grad_gated * out_gain * gating, mixed_normed, inv_mixed)
        grad_mixed_low = jnp.where(valid, grad_mixed, 0.0).astype(BF)
        grad_mixed_s[here, :] = grad_mixed_low
        for h in range(heads):
            lanes = slice(h * head_dim, (h + 1) * head_dim)
            grad_weights = dot_nt(grad_mixed_low[:, lanes], vqk_ref[0, :ends, lanes])
            grad_scores = grad_weights * score_slope_ref[h, here, :ends]
            diag_ref[h, :, first:] += grad_scores
            grad_scores_low = grad_scores.astype(BF)
            grads_s[h, here, :ends] = grad_scores_low
            grad_query = dot_nn(grad_scores_low, vqk_ref[2, :ends, lanes]) * scale
            proj_grad_s[2, here, lanes] = (grad_query * slope_ref[2, here, lanes]).astype(BF)
    gain_ref[...] = grad_out_gain

    for j in range(size):
        here = slice(j * rows, (j + 1) * rows)
        later = slice(j * rows, total)
        for h in range(heads):
            lanes = slice(h * head_dim, (h + 1) * head_dim)
            grad_key = dot_tn(grads_s[h, later, here], vqk_ref[1, later, lanes]) * scale
            proj_grad_s[3, here, lanes] = (grad_key * slope_ref[3, here, lanes]).astype(BF)
            grad_value = dot_tn(weights_ref[h, later, here], grad_mixed_s[later, lanes])
            proj_grad_s[1, here, lanes] = (grad_value * slope_ref[1, here, lanes]).astype(BF)

    half = total // 2
    block = width // 4
    own_block = proj_grad_s[me]
    cot_block = cot_s[:, pl.ds(pl.multiple_of(me * block, block), block)]
    for ref, side in ((send_ref, 1 - core), (keep_ref, core)):
        lanes = pl.ds(pl.multiple_of(side * half, half), half)
        uvqk_term = dot_tn(scaled_ref[:, lanes], own_block)
        for b in range(4):
            ref[b * half : (b + 1) * half, :] = uvqk_term[:, b * block : (b + 1) * block].astype(
                ref.dtype
            )
        out_term = dot_tn(gated_s[:, lanes], cot_block)
        ref[4 * half : 5 * half, :] = out_term.astype(ref.dtype)
    own_rows = pl.ds(pl.multiple_of(me * rows, rows), rows)
    own_gated_ref[...] = gated_s[own_rows, :]
    for part in range(4):
        own_grad_ref[part] = proj_grad_s[part, own_rows, :]


def rows_kernel(
    own_ref,
    own_cot_ref,
    in_gain_ref,
    uvqk_ref,
    out_w_ref,
    own_gated_ref,
    own_grad_ref,
    diag_ref,
    gain_ref,
    onehot_ref,
    output_ref,
    grad_input_ref,
    small_ref,
):
    rows, width = own_ref.shape
    heads, _, total = diag_ref.shape
    buckets, span = onehot_ref.shape
    me = lax.axis_index("seq")
    in_gain = in_gain_ref[...]
    wide = own_ref[...].astype(F32)
    normed, inv_in = normalize(wide)
    grad_scaled = jnp.zeros((rows, width), F32)
    for part in range(4):
        grad_scaled = grad_scaled + dot_nt(
            own_grad_ref[part], uvqk_ref[:, part * width : (part + 1) * width]
        )
    grad_in_gain = jnp.sum(grad_scaled * normed, axis=0, keepdims=True)
    grad_input = own_cot_ref[...].astype(F32) + norm_backward(grad_scaled * in_gain, normed, inv_in)
    grad_input_ref[...] = grad_input.astype(BF)
    output_ref[...] = (wide + dot_nn(own_gated_ref[...], out_w_ref[...])).astype(BF)

    onehot = onehot_ref[...]
    bias_sums = []
    for h in range(heads):
        folded = jnp.concatenate([diag_ref[h], jnp.zeros((rows, span - total), F32)], axis=1)
        count = rows // 2
        while count >= 8:
            folded = folded[:count, :] + pltpu.roll(folded[count:, :], span - count, 1)
            count //= 2
        while count >= 1:
            folded = folded + pltpu.roll(pltpu.roll(folded, 8 - count, 0), span - count, 1)
            count //= 2
        bias_sums.append(folded[:1, :])
    bias_sums = jnp.concatenate(bias_sums + [jnp.zeros((8 - heads, span), F32)], axis=0)
    grad_bias = sum(dot_nt(part, onehot) for part in three_parts(bias_sums))[:heads, :]
    small = jnp.concatenate(
        [
            grad_bias,
            as_rows(grad_in_gain, 4),
            as_rows(gain_ref[...], 4),
            jnp.zeros((4, buckets), F32),
        ],
        axis=0,
    )
    row = lax.broadcasted_iota(jnp.int32, small.shape, 0)
    mine = (row == me) | ((row >= 4) & (row < 8)) | (row == 8 + me)
    small_ref[...] = jnp.where(mine, small, 0.0)


def after_core_kernel(keep_ref, got_ref, small_ref, own_ref, *others):
    half = keep_ref.shape[0] // 5
    part = half // 4
    index = square_index()
    for ref, step in zip((own_ref,) + others, STEPS):
        there = jnp.bitwise_xor(index, step)
        for b in range(5):
            place = pl.ds(pl.multiple_of(b * half + there * part, part), part)
            ref[b * part : (b + 1) * part, :] = (
                keep_ref[place, :] + got_ref[place, :].astype(F32)
            ).astype(ref.dtype)
        small = jnp.where(there == 0, small_ref[...], 0.0)
        ref[5 * part :, :] = small.astype(ref.dtype)


def square_sum_kernel(own_ref, one_ref, three_ref, two_ref, sum_ref):
    body = own_ref.shape[0] - 16
    got = lambda ref, place: ref[place, :].astype(F32)
    for place, own in (
        (slice(0, body), own_ref[:body, :]),
        (slice(body, None), own_ref[body:, :].astype(BF).astype(F32)),
    ):
        sum_ref[place, :] = (
            (own + got(two_ref, place)) + (got(one_ref, place) + got(three_ref, place))
        ).astype(BF)


def pair_sum_kernel(left_ref, right_ref, sum_ref):
    sum_ref[...] = (left_ref[...].astype(F32) + right_ref[...].astype(F32)).astype(BF)


def four_sum_kernel(own_ref, one_ref, three_ref, two_ref, sum_ref):
    sum_ref[...] = (
        (own_ref[...].astype(F32) + two_ref[...].astype(F32))
        + (one_ref[...].astype(F32) + three_ref[...].astype(F32))
    ).astype(BF)


def join_kernel(*refs):
    joined = refs[-1]
    size = refs[0].shape[0]
    for n, ref in enumerate(refs[:-1]):
        joined[n * size : (n + 1) * size, :] = ref[...]


def unpack(factor, sources, kept, *refs):
    blocks = refs[: len(sources)]
    uvqk_hbm, out_hbm, wide_s, narrow_s, sems = refs[len(sources) + kept :]
    size = blocks[0].shape[0] // 4
    part = (size - 16) // 5
    width = uvqk_hbm.shape[1] // 4
    block = width // 4
    batch = lax.axis_index("batch")
    core = lax.rem(batch, 2)
    x = lax.axis_index("seq")
    index = square_index()
    copies = []
    for n, (ref, (other, second)) in enumerate(zip(blocks, sources)):
        from_core = 1 - core if other else core
        x_first = from_core == 1
        for m, first in enumerate(STEPS):
            slot = n * 4 + m
            from_x = lax.rem(x + 4 - jnp.where(x_first, first, second), 4)
            from_index = jnp.bitwise_xor(index, jnp.where(x_first, second, first))
            start = m * size
            for b in range(4):
                wide_s[slot, :, b * block : (b + 1) * block] = (
                    ref[start + b * part : start + (b + 1) * part, :].astype(F32) * factor
                )
            narrow_s[slot] = ref[start + 4 * part : start + 5 * part, :].astype(F32) * factor
            place = pl.ds(pl.multiple_of((from_core * 4 + from_index) * part, part), part)
            for copy in (
                pltpu.make_async_copy(
                    wide_s.at[slot],
                    uvqk_hbm.at[place, pl.ds(pl.multiple_of(from_x * width, width), width)],
                    sems.at[slot, 0],
                ),
                pltpu.make_async_copy(
                    narrow_s.at[slot],
                    out_hbm.at[place, pl.ds(pl.multiple_of(from_x * block, block), block)],
                    sems.at[slot, 1],
                ),
            ):
                copy.start()
                copies.append(copy)
    return copies


def unpack_kernel(factor, sources, kept, *refs):
    for copy in unpack(factor, sources, kept, *refs):
        copy.wait()


def last_kernel(factor, sources, kept, *refs):
    blocks = refs[:8]
    unpacked = refs[8 - len(sources) : 8 + kept]
    uvqk_hbm, out_hbm, bias_ref, in_gain_ref, out_gain_ref = refs[8 + kept : 13 + kept]
    copies = unpack(factor, sources, kept, *unpacked, uvqk_hbm, out_hbm, *refs[13 + kept :])
    size = blocks[0].shape[0] // 4
    core = lax.rem(lax.axis_index("batch"), 2)

    def piece(ref, first):
        return ref[(first + 1) * size - 16 : (first + 1) * size, :].astype(F32)

    def over_x(own, x_first):
        by_first = [sum(piece(ref, n) for ref in own) for n in range(4)]
        by_second = [sum(piece(ref, n) for n in range(4)) for ref in own]
        zero, one, three, two = [
            jnp.where(x_first, left, right) for left, right in zip(by_first, by_second)
        ]
        return (zero + two) + (one + three)

    summed = (over_x(blocks[:4], core == 1) + over_x(blocks[4:], core == 0)) * factor
    bias_ref[...] = summed[:4, :]
    in_gain_ref[...] = summed[4:8, :]
    out_gain_ref[...] = summed[8:12, :]
    for copy in copies:
        copy.wait()


def params(limit):
    return pltpu.CompilerParams(vmem_limit_bytes=limit)


def cost(flops, bytes_accessed):
    return pl.CostEstimate(flops=flops, bytes_accessed=bytes_accessed, transcendentals=0)


def shards(
    history,
    out_cotangent,
    lengths,
    bucket_of,
    position_bias,
    norm_gain,
    uvqk_weight,
    out_gain,
    out_weight,
):
    rows, width = history.shape[1:]
    heads, buckets = position_bias.shape
    seq_size = lax.axis_size("seq")
    batch_size = lax.axis_size("batch")
    total = rows * seq_size
    span = total + rows
    z_size = batch_size // 8
    factor = 1.0 / math.sqrt(batch_size * total)

    def along_x(values, step):
        return lax.ppermute(values, "seq", [(i, (i + step) % seq_size) for i in range(seq_size)])

    def place_of(b):
        return b // (2 * z_size), (b // 2) % z_size, b % 2

    def along_batch(values, move):
        pairs = []
        for b in range(batch_size):
            y, z, c = move(*place_of(b))
            pairs.append((b, (y * z_size + z) * 2 + c))
        return lax.ppermute(values, "batch", pairs)

    def in_square(y, z, step):
        return y ^ (step // 2), z ^ (step % 2)

    def in_shifted_square(y, z, step):
        y, z = in_square(y + 1, z + 1, step)
        return (y - 1) % 4, (z - 1) % z_size

    def far(z):
        return (z + (5 if z % 2 else 3)) % z_size

    def across(values):
        return along_batch(values, lambda y, z, c: (y, z, 1 - c))

    def along_either(values, step, x_core):
        pairs = []
        for x in range(seq_size):
            for b in range(batch_size):
                y, z, c = place_of(b)
                to_x, to_y, to_z = x, y, z
                if c == x_core:
                    to_x = (x + step) % 4
                else:
                    to_y, to_z = in_square(y, z, step)
                pairs.append(
                    (x * batch_size + b, to_x * batch_size + (to_y * z_size + to_z) * 2 + c)
                )
        return lax.ppermute(values, ("seq", "batch"), pairs)

    shape = jax.ShapeDtypeStruct
    vmem = pl.BlockSpec(memory_space=pltpu.VMEM)
    smem = pl.BlockSpec(memory_space=pltpu.SMEM)
    hbm = pl.BlockSpec(memory_space=pltpu.HBM)
    own_history = history[0]
    own_cotangent = out_cotangent[0]
    pieces = [along_x(own_history, step) for step in STEPS[1:]]
    own, own_cot, in_gain, gain, uvqk, out_w, tile, onehot = pl.pallas_call(
        prepare_kernel,
        out_shape=[
            shape((rows, width), BF),
            shape((rows, width), BF),
            shape((1, width), F32),
            shape((1, width), F32),
            shape(uvqk_weight.shape, BF),
            shape(out_weight.shape, BF),
            shape((heads, rows, total), F32),
            shape((buckets, span), BF),
        ],
        in_specs=[hbm] * 8,
        out_specs=[vmem] * 8,
        scratch_shapes=[
            pltpu.VMEM((1, total), jnp.int32),
            pltpu.VMEM((heads, buckets), F32),
            pltpu.SemaphoreType.DMA((8,)),
        ],
        compiler_params=params(SMALL),
        cost_estimate=cost(10**9, 3 * 10**6),
        name="prepare",
    )(
        *[
            pltpu.with_memory_space_constraint(values, pltpu.HBM)
            for values in (
                bucket_of.reshape(1, total),
                position_bias,
                own_history,
                own_cotangent,
                norm_gain.reshape(1, width),
                out_gain.reshape(1, width),
                uvqk_weight,
                out_weight,
            )
        ]
    )
    cot_pieces = [along_x(own_cot, step) for step in STEPS[1:]]
    scaled, gate, slope, vqk, weights, score_slope, mixed = pl.pallas_call(
        functools.partial(forward_kernel, seq_size),
        out_shape=[
            shape((total, width), BF),
            shape((total, width), F32),
            shape((4, total, width), F32),
            shape((3, total, width), BF),
            shape((heads, total, total), BF),
            shape((heads, total, total), F32),
            shape((total, width), F32),
        ],
        scratch_shapes=[pltpu.VMEM((total, width), BF)],
        compiler_params=params(LARGE),
        cost_estimate=cost(4 * 10**9, 10**7),
        name="forward",
    )(own, *pieces, tile, in_gain, uvqk)
    half = total // 2
    body = 5 * half
    send, keep, own_gated, own_grad, diag, gain_term = pl.pallas_call(
        functools.partial(backward_kernel, seq_size),
        out_shape=[
            shape((body, buckets), BF),
            shape((body, buckets), F32),
            shape((rows, width), BF),
            shape((4, rows, width), BF),
            shape((heads, rows, total), F32),
            shape((1, width), F32),
        ],
        in_specs=[smem] + [vmem] * 13,
        out_specs=[vmem] * 6,
        scratch_shapes=[
            pltpu.VMEM((total, width), BF),
            pltpu.VMEM((total, width), BF),
            pltpu.VMEM((heads, total, total), BF),
            pltpu.VMEM((total, width), BF),
            pltpu.VMEM((4, total, width), BF),
        ],
        compiler_params=params(LARGE),
        cost_estimate=cost(4 * 10**9, 10**7),
        name="backward",
    )(
        lengths,
        own_cot,
        *cot_pieces,
        gain,
        out_w,
        scaled,
        gate,
        slope,
        vqk,
        weights,
        score_slope,
        mixed,
    )

    got = across(send)
    output, grad_input, small = pl.pallas_call(
        rows_kernel,
        out_shape=[
            shape((rows, width), BF),
            shape((rows, width), BF),
            shape((16, buckets), F32),
        ],
        compiler_params=params(SMALL),
        cost_estimate=cost(10**9, 3 * 10**6),
        name="rows",
    )(own, own_cot, in_gain, uvqk, out_w, own_gated, own_grad, diag, gain_term, onehot)

    part = half // 4
    size = 5 * part + 16
    chunk = (size, buckets)
    mine, *parts = pl.pallas_call(
        after_core_kernel,
        out_shape=[shape(chunk, F32)] + [shape(chunk, BF)] * 3,
        compiler_params=params(SMALL),
        name="after_core",
    )(keep, got, small)
    parts = [
        along_batch(values, lambda y, z, c: (*in_square(y, z, step), c))
        for values, step in zip(parts, STEPS[1:])
    ]
    summed = pl.pallas_call(
        square_sum_kernel,
        out_shape=shape(chunk, BF),
        compiler_params=params(SMALL),
        name="square_sum",
    )(mine, *parts)
    parts = [
        along_batch(summed, lambda y, z, c: (*in_shifted_square(y, z, step), c))
        for step in STEPS[1:]
    ]
    summed = pl.pallas_call(
        four_sum_kernel, out_shape=shape(chunk, BF), compiler_params=params(SMALL), name="four_sum"
    )(summed, *parts)
    other = along_batch(summed, lambda y, z, c: (y, far(z), c))
    summed = pl.pallas_call(
        pair_sum_kernel, out_shape=shape(chunk, BF), compiler_params=params(SMALL), name="pair_sum"
    )(summed, other)

    blocks = [along_either(summed, step, 1) for step in STEPS[1:]]
    joined = pl.pallas_call(
        join_kernel,
        out_shape=shape((4 * size, buckets), BF),
        compiler_params=params(SMALL),
        name="join",
    )(summed, *blocks)
    columns, others = {0: joined}, {}
    def unpack_call(sources, kept, last=False):
        blocks = [(others if other else columns)[step] for other, step in sources]
        slots = 4 * len(blocks)
        outs = [shape((width, 4 * width), F32), shape((width, width), F32)]
        if last:
            blocks = [columns[step] for step in STEPS] + [others[step] for step in STEPS]
        count = len(blocks)
        return pl.pallas_call(
            functools.partial(last_kernel if last else unpack_kernel, factor, sources, len(kept)),
            out_shape=outs + [shape((4, buckets), F32)] * (3 if last else 0),
            in_specs=[vmem] * count + [hbm] * len(kept),
            out_specs=[hbm] * 2 + [vmem] * (3 if last else 0),
            input_output_aliases={count + n: n for n in range(len(kept))},
            scratch_shapes=[
                pltpu.VMEM((slots, part, width), F32),
                pltpu.VMEM((slots, part, buckets), F32),
                pltpu.SemaphoreType.DMA((slots, 2)),
            ],
            compiler_params=params(SMALL),
            cost_estimate=cost(UNPACK_FLOPS, 10**6 * slots // 4),
            name="unpack",
        )(*blocks, *kept)

    moved = {step: along_either(joined, step, 0) for step in STEPS[1:]}
    kept = unpack_call(((False, 0),), ())
    again, kept = lax.optimization_barrier((joined, kept))
    others[0] = across(again)
    for step in STEPS[1:]:
        columns[step], kept = lax.optimization_barrier((moved[step], kept))
        others[step] = across(columns[step])
    kept = unpack_call(((True, 0), (False, 1), (False, 3), (False, 2)), kept)
    grad_uvqk, grad_out_weight, grad_bias, grad_in_gain, grad_out_gain = unpack_call(
        ((True, 1), (True, 3), (True, 2)), kept, last=True
    )
    return (
        output[None],
        grad_input[None],
        grad_uvqk,
        grad_out_weight,
        grad_bias,
        grad_in_gain.reshape(width),
        grad_out_gain.reshape(width),
    )


def solution(mesh):
    return jax.shard_map(
        shards,
        mesh=mesh,
        in_specs=(
            P("batch", "seq", None),
            P("batch", "seq", None),
            P("batch"),
            P(),
            P(),
            P(),
            P(),
            P(),
            P(),
        ),
        out_specs=(P("batch", "seq", None), P("batch", "seq", None), P(), P(), P(), P(), P()),
        check_vma=False,
    )
```

```python
import functools
import math

import jax
import jax.numpy as jnp
from jax import lax
from jax.experimental import pallas as pl
from jax.experimental.pallas import tpu as pltpu
from jax.sharding import PartitionSpec as P

NORM_EPS = 1e-05
BF = jnp.bfloat16
F32 = jnp.float32
LARGE = 30 * 1024 * 1024
SMALL = 12 * 1024 * 1024
STEPS = (0, 1, 3, 2)
UNPACK_FLOPS = 10**10
FORWARD_GROUP = 4
BACKWARD_GROUP = 2
KEYS = 2
HIDDEN = -1e9


def normalize(values):
    centered = values - jnp.mean(values, axis=-1, keepdims=True)
    inv_scale = lax.rsqrt(jnp.mean(centered * centered, axis=-1, keepdims=True) + NORM_EPS)
    return (centered * inv_scale, inv_scale)


def norm_backward(grad_normed, normed, inv_scale):
    return inv_scale * (
        grad_normed
        - jnp.mean(grad_normed, axis=-1, keepdims=True)
        - normed * jnp.mean(grad_normed * normed, axis=-1, keepdims=True)
    )


def sigmoid(values):
    return 0.5 * jnp.tanh(0.5 * values) + 0.5


def dot_nn(left, right):
    return lax.dot_general(left, right, (((1,), (0,)), ((), ())), preferred_element_type=F32)


def dot_nt(left, right):
    return lax.dot_general(left, right, (((1,), (1,)), ((), ())), preferred_element_type=F32)


def dot_tn(left, right):
    return lax.dot_general(left, right, (((0,), (0,)), ((), ())), preferred_element_type=F32)


def three_parts(values):
    high = values.astype(BF)
    rest = values - high.astype(F32)
    middle = rest.astype(BF)
    low = (rest - middle.astype(F32)).astype(BF)
    return high, middle, low


def as_rows(row, parts):
    width = row.shape[1] // parts
    return jnp.concatenate([row[:, p * width : (p + 1) * width] for p in range(parts)], axis=0)


def prepare_kernel(
    bucket_hbm,
    bias_hbm,
    history_hbm,
    cotangent_hbm,
    in_gain_hbm,
    out_gain_hbm,
    uvqk_hbm,
    out_w_hbm,
    own_ref,
    own_cot_ref,
    in_gain_ref,
    out_gain_ref,
    uvqk_ref,
    out_w_ref,
    tile_ref,
    onehot_ref,
    bucket_ref,
    bias_ref,
    sems,
):
    copies = [
        pltpu.make_async_copy(source, target, sems.at[n])
        for n, (source, target) in enumerate(
            (
                (bucket_hbm, bucket_ref),
                (bias_hbm, bias_ref),
                (history_hbm, own_ref),
                (in_gain_hbm, in_gain_ref),
                (uvqk_hbm, uvqk_ref),
                (cotangent_hbm, own_cot_ref),
                (out_gain_hbm, out_gain_ref),
                (out_w_hbm, out_w_ref),
            )
        )
    ]
    for copy in copies:
        copy.start()
    heads, buckets = bias_ref.shape
    rows = own_ref.shape[0]
    total = bucket_ref.shape[1]
    copies[0].wait()
    copies[1].wait()

    span = total + rows
    offset = total - rows
    turned = offset - lax.broadcasted_iota(jnp.int32, (total, span), 1)
    turned = jnp.where(turned < 0, turned + span, turned)
    pick = (lax.broadcasted_iota(jnp.int32, (total, span), 0) == turned).astype(F32).astype(BF)
    bucket_rows = jnp.broadcast_to(bucket_ref[...].astype(F32), (8, total)).astype(BF)
    bucket_row = dot_nn(bucket_rows, pick)[:1, :]
    column = offset - lax.broadcasted_iota(jnp.int32, (1, span), 1)
    seen = jnp.where(column < 0, column + span, column) < total
    bucket_row = jnp.where(seen, bucket_row, -1.0)
    onehot = (
        lax.broadcasted_iota(jnp.int32, (buckets, span), 0).astype(F32)
        == jnp.broadcast_to(bucket_row, (buckets, span))
    ).astype(F32).astype(BF)
    onehot_ref[...] = onehot
    bias_rows = jnp.concatenate([bias_ref[...], jnp.zeros((8 - heads, buckets), F32)], axis=0)
    by_distance = sum(dot_nn(part, onehot) for part in three_parts(bias_rows))
    by_distance = jnp.where(seen, by_distance, HIDDEN)
    for h in range(heads):
        skewed = pltpu.roll(
            jnp.broadcast_to(by_distance[h : h + 1, :], (rows, span)), 0, 1, stride=1, stride_axis=0
        )
        tile_ref[h] = skewed[:, :total]
    for copy in copies[2:]:
        copy.wait()


def square_index():
    batch = lax.axis_index("batch")
    z_size = lax.axis_size("batch") // 8
    y = batch // (2 * z_size)
    z = lax.rem(batch // 2, z_size)
    bit = lambda place: lax.rem((place + 1) // 2, 2)
    return 2 * bit(y) + bit(z)


def place_pieces(refs, target, size):
    me = lax.axis_index("seq")
    for step, ref in zip(STEPS, refs):
        source = lax.rem(me + size - step, size)
        rows = ref.shape[0]
        target[pl.ds(pl.multiple_of(source * rows, rows), rows), :] = ref[...]


def forward_kernel(size, *refs):
    pieces = refs[:size]
    (
        tile_ref,
        in_gain_ref,
        uvqk_ref,
        scaled_ref,
        gate_ref,
        slope_ref,
        vqk_ref,
        weights_ref,
        score_slope_ref,
        mixed_ref,
        hist_s,
    ) = refs[size:]
    rows, width = pieces[0].shape
    total = rows * size
    heads = tile_ref.shape[0]
    head_dim = width // heads
    scale = 1.0 / math.sqrt(head_dim)
    in_gain = in_gain_ref[...]
    place_pieces(pieces, hist_s, size)
    normed, _ = normalize(hist_s[...].astype(F32))
    scaled_ref[...] = (normed * in_gain).astype(BF)
    for part in (2, 3, 1, 0):
        projected = dot_nn(scaled_ref[...], uvqk_ref[:, part * width : (part + 1) * width])
        sig = sigmoid(projected)
        activated = projected * sig
        slope_ref[part] = sig + activated * (1.0 - sig)
        if part == 0:
            gate_ref[...] = activated
        else:
            vqk_ref[part - 1] = activated.astype(BF)
    for i in range(0, size, FORWARD_GROUP):
        here = slice(i * rows, (i + FORWARD_GROUP) * rows)
        ends = (i + FORWARD_GROUP) * rows
        for h in range(heads):
            lanes = slice(h * head_dim, (h + 1) * head_dim)
            raw = dot_nt(vqk_ref[1, here, lanes], vqk_ref[2, :ends, lanes])
            for n in range(FORWARD_GROUP):
                block = slice((i + n) * rows, (i + n + 1) * rows)
                seen = (i + n + 1) * rows
                scores = raw[n * rows : (n + 1) * rows, :seen] * scale
                scores = scores + tile_ref[h, :, total - seen :]
                sig = sigmoid(scores)
                weights = scores * sig
                score_slope_ref[h, block, :seen] = sig + weights * (1.0 - sig)
                weights_ref[h, block, :seen] = weights.astype(BF)
                if n < FORWARD_GROUP - 1:
                    weights_ref[h, block, seen:ends] = jnp.zeros((rows, ends - seen), BF)
            mixed_ref[here, lanes] = dot_nn(weights_ref[h, here, :ends], vqk_ref[0, :ends, lanes])


def backward_kernel(size, length_ref, *refs):
    pieces = refs[:size]
    (
        out_gain_ref,
        out_w_ref,
        scaled_ref,
        gate_ref,
        slope_ref,
        vqk_ref,
        weights_ref,
        score_slope_ref,
        mixed_ref,
        send_ref,
        keep_ref,
        own_gated_ref,
        own_grad_ref,
        diag_ref,
        gain_ref,
        cot_s,
        gated_s,
        grads_s,
        grad_mixed_s,
        proj_grad_s,
        grad_gated_s,
    ) = refs[size:]
    rows, width = pieces[0].shape
    total = rows * size
    heads = weights_ref.shape[0]
    head_dim = width // heads
    scale = 1.0 / math.sqrt(head_dim)
    me = lax.axis_index("seq")
    core = lax.rem(lax.axis_index("batch"), 2)
    length = length_ref[0]
    out_gain = out_gain_ref[...]
    place_pieces(pieces, cot_s, size)
    grad_out_gain = jnp.zeros((1, width), F32)
    for h in range(heads):
        diag_ref[h] = jnp.zeros((rows, total), F32)
    grad_gated_s[...] = dot_nt(cot_s[...], out_w_ref[...])
    for i in range(0, size, BACKWARD_GROUP):
        here = slice(i * rows, (i + BACKWARD_GROUP) * rows)
        ends = (i + BACKWARD_GROUP) * rows
        valid = (lax.broadcasted_iota(jnp.int32, (BACKWARD_GROUP * rows, 1), 0) + i * rows) < length
        mixed = jnp.where(valid, mixed_ref[here, :], 0.0)
        mixed_normed, inv_mixed = normalize(mixed)
        gating = gate_ref[here, :]
        gated_s[here, :] = (mixed_normed * out_gain * gating).astype(BF)
        grad_gated = grad_gated_s[here, :]
        times_normed = grad_gated * mixed_normed
        grad_out_gain = grad_out_gain + jnp.sum(times_normed * gating, axis=0, keepdims=True)
        proj_grad_s[0, here, :] = (times_normed * out_gain * slope_ref[0, here, :]).astype(BF)
        grad_mixed = norm_backward(grad_gated * out_gain * gating, mixed_normed, inv_mixed)
        grad_mixed_s[here, :] = jnp.where(valid, grad_mixed, 0.0).astype(BF)
        for h in range(heads):
            lanes = slice(h * head_dim, (h + 1) * head_dim)
            grad_weights = dot_nt(grad_mixed_s[here, lanes], vqk_ref[0, :ends, lanes])
            for n in range(BACKWARD_GROUP):
                block = slice((i + n) * rows, (i + n + 1) * rows)
                seen = (i + n + 1) * rows
                grad_scores = (
                    grad_weights[n * rows : (n + 1) * rows, :seen] * score_slope_ref[h, block, :seen]
                )
                diag_ref[h, :, total - seen :] += grad_scores
                grads_s[h, block, :seen] = grad_scores.astype(BF)
                if n < BACKWARD_GROUP - 1:
                    grads_s[h, block, seen:ends] = jnp.zeros((rows, ends - seen), BF)
            grad_query = dot_nn(grads_s[h, here, :ends], vqk_ref[2, :ends, lanes]) * scale
            proj_grad_s[2, here, lanes] = (grad_query * slope_ref[2, here, lanes]).astype(BF)
    gain_ref[...] = grad_out_gain

    for j in range(0, size, KEYS):
        here = slice(j * rows, (j + KEYS) * rows)
        later = slice(j * rows, total)
        for h in range(heads):
            lanes = slice(h * head_dim, (h + 1) * head_dim)
            grad_key = dot_tn(grads_s[h, later, here], vqk_ref[1, later, lanes]) * scale
            proj_grad_s[3, here, lanes] = (grad_key * slope_ref[3, here, lanes]).astype(BF)
            grad_value = dot_tn(weights_ref[h, later, here], grad_mixed_s[later, lanes])
            proj_grad_s[1, here, lanes] = (grad_value * slope_ref[1, here, lanes]).astype(BF)

    half = total // 2
    block = width // 4
    own_block = proj_grad_s[me]
    cot_block = cot_s[:, pl.ds(pl.multiple_of(me * block, block), block)]
    for ref, side in ((send_ref, 1 - core), (keep_ref, core)):
        lanes = pl.ds(pl.multiple_of(side * half, half), half)
        uvqk_term = dot_tn(scaled_ref[:, lanes], own_block)
        for b in range(4):
            ref[b * half : (b + 1) * half, :] = uvqk_term[:, b * block : (b + 1) * block].astype(
                ref.dtype
            )
        out_term = dot_tn(gated_s[:, lanes], cot_block)
        ref[4 * half : 5 * half, :] = out_term.astype(ref.dtype)
    own_rows = pl.ds(pl.multiple_of(me * rows, rows), rows)
    own_gated_ref[...] = gated_s[own_rows, :]
    for part in range(4):
        own_grad_ref[part] = proj_grad_s[part, own_rows, :]


def rows_kernel(
    own_ref, own_cot_ref, in_gain_ref, out_w_ref, own_gated_ref, scaled_ref, output_ref, grad_ref
):
    wide = own_ref[...].astype(F32)
    normed, inv_in = normalize(wide)
    grad_normed = scaled_ref[...] * in_gain_ref[...]
    grad_input = own_cot_ref[...].astype(F32) + norm_backward(grad_normed, normed, inv_in)
    grad_ref[...] = grad_input.astype(BF)
    output_ref[...] = (wide + dot_nn(own_gated_ref[...], out_w_ref[...])).astype(BF)


def small_kernel(
    own_ref, uvqk_ref, own_grad_ref, diag_ref, gain_ref, onehot_ref, scaled_ref, small_ref
):
    rows, width = own_ref.shape
    heads, _, total = diag_ref.shape
    buckets, span = onehot_ref.shape
    me = lax.axis_index("seq")
    normed, _ = normalize(own_ref[...].astype(F32))
    grad_scaled = jnp.zeros((rows, width), F32)
    for part in range(4):
        grad_scaled = grad_scaled + dot_nt(
            own_grad_ref[part], uvqk_ref[:, part * width : (part + 1) * width]
        )
    grad_in_gain = jnp.sum(grad_scaled * normed, axis=0, keepdims=True)
    scaled_ref[...] = grad_scaled

    onehot = onehot_ref[...]
    bias_sums = []
    for h in range(heads):
        folded = jnp.concatenate([diag_ref[h], jnp.zeros((rows, span - total), F32)], axis=1)
        count = rows // 2
        while count >= 8:
            folded = folded[:count, :] + pltpu.roll(folded[count:, :], span - count, 1)
            count //= 2
        while count >= 1:
            folded = folded + pltpu.roll(pltpu.roll(folded, 8 - count, 0), span - count, 1)
            count //= 2
        bias_sums.append(folded[:1, :])
    bias_sums = jnp.concatenate(bias_sums + [jnp.zeros((8 - heads, span), F32)], axis=0)
    grad_bias = sum(dot_nt(part, onehot) for part in three_parts(bias_sums))[:heads, :]
    small = jnp.concatenate(
        [
            grad_bias,
            as_rows(grad_in_gain, 4),
            as_rows(gain_ref[...], 4),
            jnp.zeros((4, buckets), F32),
        ],
        axis=0,
    )
    row = lax.broadcasted_iota(jnp.int32, small.shape, 0)
    mine = (row == me) | ((row >= 4) & (row < 8)) | (row == 8 + me)
    small_ref[...] = jnp.where(mine, small, 0.0)


def after_core_kernel(keep_ref, got_ref, small_ref, own_ref, *others):
    half = keep_ref.shape[0] // 5
    part = half // 4
    index = square_index()
    for ref, step in zip((own_ref,) + others, STEPS):
        there = jnp.bitwise_xor(index, step)
        for b in range(5):
            place = pl.ds(pl.multiple_of(b * half + there * part, part), part)
            ref[b * part : (b + 1) * part, :] = (
                keep_ref[place, :] + got_ref[place, :].astype(F32)
            ).astype(ref.dtype)
        small = jnp.where(there == 0, small_ref[...], 0.0)
        ref[5 * part :, :] = small.astype(ref.dtype)


def square_sum_kernel(own_ref, one_ref, three_ref, two_ref, sum_ref):
    body = own_ref.shape[0] - 16
    got = lambda ref, place: ref[place, :].astype(F32)
    for place, own in (
        (slice(0, body), own_ref[:body, :]),
        (slice(body, None), own_ref[body:, :].astype(BF).astype(F32)),
    ):
        sum_ref[place, :] = (
            (own + got(two_ref, place)) + (got(one_ref, place) + got(three_ref, place))
        ).astype(BF)


def pair_sum_kernel(left_ref, right_ref, sum_ref):
    sum_ref[...] = (left_ref[...].astype(F32) + right_ref[...].astype(F32)).astype(BF)


def four_sum_kernel(own_ref, one_ref, three_ref, two_ref, sum_ref):
    sum_ref[...] = (
        (own_ref[...].astype(F32) + two_ref[...].astype(F32))
        + (one_ref[...].astype(F32) + three_ref[...].astype(F32))
    ).astype(BF)


def join_kernel(*refs):
    joined = refs[-1]
    size = refs[0].shape[0]
    for n, ref in enumerate(refs[:-1]):
        joined[n * size : (n + 1) * size, :] = ref[...]


def unpack(factor, sources, kept, *refs):
    blocks = refs[: len(sources)]
    uvqk_hbm, out_hbm, wide_s, narrow_s, sems = refs[len(sources) + kept :]
    size = blocks[0].shape[0] // 4
    part = (size - 16) // 5
    width = uvqk_hbm.shape[1] // 4
    block = width // 4
    batch = lax.axis_index("batch")
    core = lax.rem(batch, 2)
    x = lax.axis_index("seq")
    index = square_index()
    copies = []
    for n, (ref, (other, second)) in enumerate(zip(blocks, sources)):
        from_core = 1 - core if other else core
        x_first = from_core == 1
        for m, first in enumerate(STEPS):
            slot = n * 4 + m
            from_x = lax.rem(x + 4 - jnp.where(x_first, first, second), 4)
            from_index = jnp.bitwise_xor(index, jnp.where(x_first, second, first))
            start = m * size
            for b in range(4):
                wide_s[slot, :, b * block : (b + 1) * block] = (
                    ref[start + b * part : start + (b + 1) * part, :].astype(F32) * factor
                )
            narrow_s[slot] = ref[start + 4 * part : start + 5 * part, :].astype(F32) * factor
            place = pl.ds(pl.multiple_of((from_core * 4 + from_index) * part, part), part)
            for copy in (
                pltpu.make_async_copy(
                    wide_s.at[slot],
                    uvqk_hbm.at[place, pl.ds(pl.multiple_of(from_x * width, width), width)],
                    sems.at[slot, 0],
                ),
                pltpu.make_async_copy(
                    narrow_s.at[slot],
                    out_hbm.at[place, pl.ds(pl.multiple_of(from_x * block, block), block)],
                    sems.at[slot, 1],
                ),
            ):
                copy.start()
                copies.append(copy)
    return copies


def unpack_kernel(factor, sources, kept, *refs):
    for copy in unpack(factor, sources, kept, *refs):
        copy.wait()


def last_kernel(factor, sources, kept, *refs):
    blocks = refs[:8]
    unpacked = refs[8 - len(sources) : 8 + kept]
    uvqk_hbm, out_hbm, bias_ref, in_gain_ref, out_gain_ref = refs[8 + kept : 13 + kept]
    copies = unpack(factor, sources, kept, *unpacked, uvqk_hbm, out_hbm, *refs[13 + kept :])
    size = blocks[0].shape[0] // 4
    core = lax.rem(lax.axis_index("batch"), 2)

    def piece(ref, first):
        return ref[(first + 1) * size - 16 : (first + 1) * size, :].astype(F32)

    def over_x(own, x_first):
        by_first = [sum(piece(ref, n) for ref in own) for n in range(4)]
        by_second = [sum(piece(ref, n) for n in range(4)) for ref in own]
        zero, one, three, two = [
            jnp.where(x_first, left, right) for left, right in zip(by_first, by_second)
        ]
        return (zero + two) + (one + three)

    summed = (over_x(blocks[:4], core == 1) + over_x(blocks[4:], core == 0)) * factor
    bias_ref[...] = summed[:4, :]
    in_gain_ref[...] = summed[4:8, :]
    out_gain_ref[...] = summed[8:12, :]
    for copy in copies:
        copy.wait()


def params(limit):
    return pltpu.CompilerParams(vmem_limit_bytes=limit)


def cost(flops, bytes_accessed):
    return pl.CostEstimate(flops=flops, bytes_accessed=bytes_accessed, transcendentals=0)


def shards(
    history,
    out_cotangent,
    lengths,
    bucket_of,
    position_bias,
    norm_gain,
    uvqk_weight,
    out_gain,
    out_weight,
):
    rows, width = history.shape[1:]
    heads, buckets = position_bias.shape
    seq_size = lax.axis_size("seq")
    batch_size = lax.axis_size("batch")
    total = rows * seq_size
    span = total + rows
    z_size = batch_size // 8
    factor = 1.0 / math.sqrt(batch_size * total)

    def along_x(values, step):
        return lax.ppermute(values, "seq", [(i, (i + step) % seq_size) for i in range(seq_size)])

    def place_of(b):
        return b // (2 * z_size), (b // 2) % z_size, b % 2

    def along_batch(values, move):
        pairs = []
        for b in range(batch_size):
            y, z, c = move(*place_of(b))
            pairs.append((b, (y * z_size + z) * 2 + c))
        return lax.ppermute(values, "batch", pairs)

    def in_square(y, z, step):
        return y ^ (step // 2), z ^ (step % 2)

    def in_shifted_square(y, z, step):
        y, z = in_square(y + 1, z + 1, step)
        return (y - 1) % 4, (z - 1) % z_size

    def far(z):
        return (z + (5 if z % 2 else 3)) % z_size

    def across(values):
        return along_batch(values, lambda y, z, c: (y, z, 1 - c))

    def along_either(values, step, x_core):
        pairs = []
        for x in range(seq_size):
            for b in range(batch_size):
                y, z, c = place_of(b)
                to_x, to_y, to_z = x, y, z
                if c == x_core:
                    to_x = (x + step) % 4
                else:
                    to_y, to_z = in_square(y, z, step)
                pairs.append(
                    (x * batch_size + b, to_x * batch_size + (to_y * z_size + to_z) * 2 + c)
                )
        return lax.ppermute(values, ("seq", "batch"), pairs)

    shape = jax.ShapeDtypeStruct
    vmem = pl.BlockSpec(memory_space=pltpu.VMEM)
    smem = pl.BlockSpec(memory_space=pltpu.SMEM)
    hbm = pl.BlockSpec(memory_space=pltpu.HBM)
    own_history = history[0]
    own_cotangent = out_cotangent[0]
    pieces = [along_x(own_history, step) for step in STEPS[1:]]
    own, own_cot, in_gain, gain, uvqk, out_w, tile, onehot = pl.pallas_call(
        prepare_kernel,
        out_shape=[
            shape((rows, width), BF),
            shape((rows, width), BF),
            shape((1, width), F32),
            shape((1, width), F32),
            shape(uvqk_weight.shape, BF),
            shape(out_weight.shape, BF),
            shape((heads, rows, total), F32),
            shape((buckets, span), BF),
        ],
        in_specs=[hbm] * 8,
        out_specs=[vmem] * 8,
        scratch_shapes=[
            pltpu.VMEM((1, total), jnp.int32),
            pltpu.VMEM((heads, buckets), F32),
            pltpu.SemaphoreType.DMA((8,)),
        ],
        compiler_params=params(SMALL),
        cost_estimate=cost(10**9, 3 * 10**6),
        name="prepare",
    )(
        *[
            pltpu.with_memory_space_constraint(values, pltpu.HBM)
            for values in (
                bucket_of.reshape(1, total),
                position_bias,
                own_history,
                own_cotangent,
                norm_gain.reshape(1, width),
                out_gain.reshape(1, width),
                uvqk_weight,
                out_weight,
            )
        ]
    )
    cot_pieces = [along_x(own_cot, step) for step in STEPS[1:]]
    scaled, gate, slope, vqk, weights, score_slope, mixed = pl.pallas_call(
        functools.partial(forward_kernel, seq_size),
        out_shape=[
            shape((total, width), BF),
            shape((total, width), F32),
            shape((4, total, width), F32),
            shape((3, total, width), BF),
            shape((heads, total, total), BF),
            shape((heads, total, total), F32),
            shape((total, width), F32),
        ],
        scratch_shapes=[pltpu.VMEM((total, width), BF)],
        compiler_params=params(LARGE),
        cost_estimate=cost(4 * 10**9, 10**7),
        name="forward",
    )(own, *pieces, tile, in_gain, uvqk)
    half = total // 2
    body = 5 * half
    send, keep, own_gated, own_grad, diag, gain_term = pl.pallas_call(
        functools.partial(backward_kernel, seq_size),
        out_shape=[
            shape((body, buckets), BF),
            shape((body, buckets), F32),
            shape((rows, width), BF),
            shape((4, rows, width), BF),
            shape((heads, rows, total), F32),
            shape((1, width), F32),
        ],
        in_specs=[smem] + [vmem] * 13,
        out_specs=[vmem] * 6,
        scratch_shapes=[
            pltpu.VMEM((total, width), BF),
            pltpu.VMEM((total, width), BF),
            pltpu.VMEM((heads, total, total), BF),
            pltpu.VMEM((total, width), BF),
            pltpu.VMEM((4, total, width), BF),
            pltpu.VMEM((total, width), F32),
        ],
        compiler_params=params(LARGE),
        cost_estimate=cost(4 * 10**9, 10**7),
        name="backward",
    )(
        lengths,
        own_cot,
        *cot_pieces,
        gain,
        out_w,
        scaled,
        gate,
        slope,
        vqk,
        weights,
        score_slope,
        mixed,
    )

    got = across(send)
    grad_scaled, small = pl.pallas_call(
        small_kernel,
        out_shape=[shape((rows, width), F32), shape((16, buckets), F32)],
        compiler_params=params(SMALL),
        cost_estimate=cost(10**9, 3 * 10**6),
        name="small",
    )(own, uvqk, own_grad, diag, gain_term, onehot)

    part = half // 4
    size = 5 * part + 16
    chunk = (size, buckets)
    mine, *parts = pl.pallas_call(
        after_core_kernel,
        out_shape=[shape(chunk, F32)] + [shape(chunk, BF)] * 3,
        compiler_params=params(SMALL),
        name="after_core",
    )(keep, got, small)
    grad_scaled, mine, *parts = lax.optimization_barrier((grad_scaled, mine, *parts))
    output, grad_input = pl.pallas_call(
        rows_kernel,
        out_shape=[shape((rows, width), BF), shape((rows, width), BF)],
        compiler_params=params(SMALL),
        cost_estimate=cost(2 * 10**9, 3 * 10**6),
        name="rows",
    )(own, own_cot, in_gain, out_w, own_gated, grad_scaled)
    parts = [
        along_batch(values, lambda y, z, c: (*in_square(y, z, step), c))
        for values, step in zip(parts, STEPS[1:])
    ]
    summed = pl.pallas_call(
        square_sum_kernel,
        out_shape=shape(chunk, BF),
        compiler_params=params(SMALL),
        name="square_sum",
    )(mine, *parts)
    parts = [
        along_batch(summed, lambda y, z, c: (*in_shifted_square(y, z, step), c))
        for step in STEPS[1:]
    ]
    summed = pl.pallas_call(
        four_sum_kernel, out_shape=shape(chunk, BF), compiler_params=params(SMALL), name="four_sum"
    )(summed, *parts)
    other = along_batch(summed, lambda y, z, c: (y, far(z), c))
    summed = pl.pallas_call(
        pair_sum_kernel, out_shape=shape(chunk, BF), compiler_params=params(SMALL), name="pair_sum"
    )(summed, other)

    blocks = [along_either(summed, step, 1) for step in STEPS[1:]]
    joined = pl.pallas_call(
        join_kernel,
        out_shape=shape((4 * size, buckets), BF),
        compiler_params=params(SMALL),
        name="join",
    )(summed, *blocks)
    columns, others = {0: joined}, {}
    def unpack_call(sources, kept, last=False):
        blocks = [(others if other else columns)[step] for other, step in sources]
        slots = 4 * len(blocks)
        outs = [shape((width, 4 * width), F32), shape((width, width), F32)]
        if last:
            blocks = [columns[step] for step in STEPS] + [others[step] for step in STEPS]
        count = len(blocks)
        return pl.pallas_call(
            functools.partial(last_kernel if last else unpack_kernel, factor, sources, len(kept)),
            out_shape=outs + [shape((4, buckets), F32)] * (3 if last else 0),
            in_specs=[vmem] * count + [hbm] * len(kept),
            out_specs=[hbm] * 2 + [vmem] * (3 if last else 0),
            input_output_aliases={count + n: n for n in range(len(kept))},
            scratch_shapes=[
                pltpu.VMEM((slots, part, width), F32),
                pltpu.VMEM((slots, part, buckets), F32),
                pltpu.SemaphoreType.DMA((slots, 2)),
            ],
            compiler_params=params(SMALL),
            cost_estimate=cost(UNPACK_FLOPS, 10**6 * slots // 4),
            name="unpack",
        )(*blocks, *kept)

    moved = {step: along_either(joined, step, 0) for step in STEPS[1:]}
    kept = unpack_call(((False, 0),), ())
    again, kept = lax.optimization_barrier((joined, kept))
    others[0] = across(again)
    for step in STEPS[1:]:
        columns[step], kept = lax.optimization_barrier((moved[step], kept))
        others[step] = across(columns[step])
    kept = unpack_call(((True, 0), (False, 1), (False, 3), (False, 2)), kept)
    grad_uvqk, grad_out_weight, grad_bias, grad_in_gain, grad_out_gain = unpack_call(
        ((True, 1), (True, 3), (True, 2)), kept, last=True
    )
    return (
        output[None],
        grad_input[None],
        grad_uvqk,
        grad_out_weight,
        grad_bias,
        grad_in_gain.reshape(width),
        grad_out_gain.reshape(width),
    )


def solution(mesh):
    return jax.shard_map(
        shards,
        mesh=mesh,
        in_specs=(
            P("batch", "seq", None),
            P("batch", "seq", None),
            P("batch"),
            P(),
            P(),
            P(),
            P(),
            P(),
            P(),
        ),
        out_specs=(P("batch", "seq", None), P("batch", "seq", None), P(), P(), P(), P(), P()),
        check_vma=False,
    )
```

```python
import functools
import math

import jax
import jax.numpy as jnp
from jax import lax
from jax.experimental import pallas as pl
from jax.experimental.pallas import tpu as pltpu
from jax.sharding import PartitionSpec as P

NORM_EPS = 1e-05
BF = jnp.bfloat16
F32 = jnp.float32
LARGE = 30 * 1024 * 1024
SMALL = 12 * 1024 * 1024
STEPS = (0, 1, 3, 2)
UNPACK_FLOPS = 10**10
FORWARD_GROUP = 4
BACKWARD_GROUP = 4
KEYS = 2
HIDDEN = -1e9


def normalize(values):
    centered = values - jnp.mean(values, axis=-1, keepdims=True)
    inv_scale = lax.rsqrt(jnp.mean(centered * centered, axis=-1, keepdims=True) + NORM_EPS)
    return (centered * inv_scale, inv_scale)


def norm_backward(grad_normed, normed, inv_scale):
    return inv_scale * (
        grad_normed
        - jnp.mean(grad_normed, axis=-1, keepdims=True)
        - normed * jnp.mean(grad_normed * normed, axis=-1, keepdims=True)
    )


def sigmoid(values):
    return 0.5 * jnp.tanh(0.5 * values) + 0.5


def dot_nn(left, right):
    return lax.dot_general(left, right, (((1,), (0,)), ((), ())), preferred_element_type=F32)


def dot_nt(left, right):
    return lax.dot_general(left, right, (((1,), (1,)), ((), ())), preferred_element_type=F32)


def dot_tn(left, right):
    return lax.dot_general(left, right, (((0,), (0,)), ((), ())), preferred_element_type=F32)


def three_parts(values):
    high = values.astype(BF)
    rest = values - high.astype(F32)
    middle = rest.astype(BF)
    low = (rest - middle.astype(F32)).astype(BF)
    return high, middle, low


def as_rows(row, parts):
    width = row.shape[1] // parts
    return jnp.concatenate([row[:, p * width : (p + 1) * width] for p in range(parts)], axis=0)


def prepare_kernel(
    bucket_hbm,
    bias_hbm,
    history_hbm,
    cotangent_hbm,
    in_gain_hbm,
    out_gain_hbm,
    uvqk_hbm,
    out_w_hbm,
    own_ref,
    own_cot_ref,
    in_gain_ref,
    out_gain_ref,
    uvqk_ref,
    out_w_ref,
    tile_ref,
    onehot_ref,
    bucket_ref,
    bias_ref,
    sems,
):
    copies = [
        pltpu.make_async_copy(source, target, sems.at[n])
        for n, (source, target) in enumerate(
            (
                (bucket_hbm, bucket_ref),
                (bias_hbm, bias_ref),
                (history_hbm, own_ref),
                (in_gain_hbm, in_gain_ref),
                (uvqk_hbm, uvqk_ref),
                (cotangent_hbm, own_cot_ref),
                (out_gain_hbm, out_gain_ref),
                (out_w_hbm, out_w_ref),
            )
        )
    ]
    for copy in copies:
        copy.start()
    heads, buckets = bias_ref.shape
    rows = own_ref.shape[0]
    total = bucket_ref.shape[1]
    copies[0].wait()
    copies[1].wait()

    span = total + rows
    offset = total - rows
    turned = offset - lax.broadcasted_iota(jnp.int32, (total, span), 1)
    turned = jnp.where(turned < 0, turned + span, turned)
    pick = (lax.broadcasted_iota(jnp.int32, (total, span), 0) == turned).astype(F32).astype(BF)
    bucket_rows = jnp.broadcast_to(bucket_ref[...].astype(F32), (8, total)).astype(BF)
    bucket_row = dot_nn(bucket_rows, pick)[:1, :]
    column = offset - lax.broadcasted_iota(jnp.int32, (1, span), 1)
    seen = jnp.where(column < 0, column + span, column) < total
    bucket_row = jnp.where(seen, bucket_row, -1.0)
    onehot = (
        lax.broadcasted_iota(jnp.int32, (buckets, span), 0).astype(F32)
        == jnp.broadcast_to(bucket_row, (buckets, span))
    ).astype(F32).astype(BF)
    onehot_ref[...] = onehot
    bias_rows = jnp.concatenate([bias_ref[...], jnp.zeros((8 - heads, buckets), F32)], axis=0)
    by_distance = sum(dot_nn(part, onehot) for part in three_parts(bias_rows))
    by_distance = jnp.where(seen, by_distance, HIDDEN)
    for h in range(heads):
        skewed = pltpu.roll(
            jnp.broadcast_to(by_distance[h : h + 1, :], (rows, span)), 0, 1, stride=1, stride_axis=0
        )
        tile_ref[h] = skewed[:, :total]
    for copy in copies[2:]:
        copy.wait()


def square_index():
    batch = lax.axis_index("batch")
    z_size = lax.axis_size("batch") // 8
    y = batch // (2 * z_size)
    z = lax.rem(batch // 2, z_size)
    bit = lambda place: lax.rem((place + 1) // 2, 2)
    return 2 * bit(y) + bit(z)


def place_pieces(refs, target, size):
    me = lax.axis_index("seq")
    for step, ref in zip(STEPS, refs):
        source = lax.rem(me + size - step, size)
        rows = ref.shape[0]
        target[pl.ds(pl.multiple_of(source * rows, rows), rows), :] = ref[...]


def forward_kernel(size, *refs):
    pieces = refs[:size]
    (
        tile_ref,
        in_gain_ref,
        uvqk_ref,
        scaled_ref,
        gate_ref,
        slope_ref,
        vqk_ref,
        weights_ref,
        score_slope_ref,
        mixed_ref,
        hist_s,
    ) = refs[size:]
    rows, width = pieces[0].shape
    total = rows * size
    heads = tile_ref.shape[0]
    head_dim = width // heads
    scale = 1.0 / math.sqrt(head_dim)
    in_gain = in_gain_ref[...]
    place_pieces(pieces, hist_s, size)
    normed, _ = normalize(hist_s[...].astype(F32))
    scaled_ref[...] = (normed * in_gain).astype(BF)
    for part in (2, 3, 1, 0):
        projected = dot_nn(scaled_ref[...], uvqk_ref[:, part * width : (part + 1) * width])
        sig = sigmoid(projected)
        activated = projected * sig
        slope_ref[part] = sig + activated * (1.0 - sig)
        if part == 0:
            gate_ref[...] = activated
        else:
            vqk_ref[part - 1] = activated.astype(BF)
    for i in range(0, size, FORWARD_GROUP):
        here = slice(i * rows, (i + FORWARD_GROUP) * rows)
        ends = (i + FORWARD_GROUP) * rows
        for h in range(heads):
            lanes = slice(h * head_dim, (h + 1) * head_dim)
            raw = dot_nt(vqk_ref[1, here, lanes], vqk_ref[2, :ends, lanes])
            for n in range(FORWARD_GROUP):
                block = slice((i + n) * rows, (i + n + 1) * rows)
                seen = (i + n + 1) * rows
                scores = raw[n * rows : (n + 1) * rows, :seen] * scale
                scores = scores + tile_ref[h, :, total - seen :]
                sig = sigmoid(scores)
                weights = scores * sig
                score_slope_ref[h, block, :seen] = sig + weights * (1.0 - sig)
                weights_ref[h, block, :seen] = weights.astype(BF)
                if n < FORWARD_GROUP - 1:
                    weights_ref[h, block, seen:ends] = jnp.zeros((rows, ends - seen), BF)
            mixed_ref[here, lanes] = dot_nn(weights_ref[h, here, :ends], vqk_ref[0, :ends, lanes])


def backward_kernel(size, length_ref, *refs):
    pieces = refs[:size]
    (
        out_gain_ref,
        out_w_ref,
        scaled_ref,
        gate_ref,
        slope_ref,
        vqk_ref,
        weights_ref,
        score_slope_ref,
        mixed_ref,
        send_ref,
        keep_ref,
        own_gated_ref,
        own_grad_ref,
        diag_ref,
        gain_ref,
        cot_s,
        gated_s,
        grads_s,
        grad_mixed_s,
        proj_grad_s,
        grad_gated_s,
    ) = refs[size:]
    rows, width = pieces[0].shape
    total = rows * size
    heads = weights_ref.shape[0]
    head_dim = width // heads
    scale = 1.0 / math.sqrt(head_dim)
    me = lax.axis_index("seq")
    core = lax.rem(lax.axis_index("batch"), 2)
    length = length_ref[0]
    out_gain = out_gain_ref[...]
    place_pieces(pieces, cot_s, size)
    grad_out_gain = jnp.zeros((1, width), F32)
    for h in range(heads):
        diag_ref[h] = jnp.zeros((rows, total), F32)
    grad_gated_s[...] = dot_nt(cot_s[...], out_w_ref[...])
    for i in range(0, size, BACKWARD_GROUP):
        here = slice(i * rows, (i + BACKWARD_GROUP) * rows)
        ends = (i + BACKWARD_GROUP) * rows
        valid = (lax.broadcasted_iota(jnp.int32, (BACKWARD_GROUP * rows, 1), 0) + i * rows) < length
        mixed = jnp.where(valid, mixed_ref[here, :], 0.0)
        mixed_normed, inv_mixed = normalize(mixed)
        gating = gate_ref[here, :]
        gated_s[here, :] = (mixed_normed * out_gain * gating).astype(BF)
        grad_gated = grad_gated_s[here, :]
        times_normed = grad_gated * mixed_normed
        grad_out_gain = grad_out_gain + jnp.sum(times_normed * gating, axis=0, keepdims=True)
        proj_grad_s[0, here, :] = (times_normed * out_gain * slope_ref[0, here, :]).astype(BF)
        grad_mixed = norm_backward(grad_gated * out_gain * gating, mixed_normed, inv_mixed)
        grad_mixed_s[here, :] = jnp.where(valid, grad_mixed, 0.0).astype(BF)
        by_head = [slice(h * head_dim, (h + 1) * head_dim) for h in range(heads)]
        products = [dot_nt(grad_mixed_s[here, lanes], vqk_ref[0, :ends, lanes]) for lanes in by_head]
        for h, grad_weights in enumerate(products):
            for n in range(BACKWARD_GROUP):
                block = slice((i + n) * rows, (i + n + 1) * rows)
                seen = (i + n + 1) * rows
                grad_scores = (
                    grad_weights[n * rows : (n + 1) * rows, :seen] * score_slope_ref[h, block, :seen]
                )
                diag_ref[h, :, total - seen :] += grad_scores
                grads_s[h, block, :seen] = grad_scores.astype(BF)
                if n < BACKWARD_GROUP - 1:
                    grads_s[h, block, seen:ends] = jnp.zeros((rows, ends - seen), BF)
        for h, lanes in enumerate(by_head):
            grad_query = dot_nn(grads_s[h, here, :ends], vqk_ref[2, :ends, lanes]) * scale
            proj_grad_s[2, here, lanes] = (grad_query * slope_ref[2, here, lanes]).astype(BF)
    gain_ref[...] = grad_out_gain

    for j in range(0, size, KEYS):
        here = slice(j * rows, (j + KEYS) * rows)
        later = slice(j * rows, total)
        for h in range(heads):
            lanes = slice(h * head_dim, (h + 1) * head_dim)
            grad_key = dot_tn(grads_s[h, later, here], vqk_ref[1, later, lanes]) * scale
            proj_grad_s[3, here, lanes] = (grad_key * slope_ref[3, here, lanes]).astype(BF)
            grad_value = dot_tn(weights_ref[h, later, here], grad_mixed_s[later, lanes])
            proj_grad_s[1, here, lanes] = (grad_value * slope_ref[1, here, lanes]).astype(BF)

    half = total // 2
    block = width // 4
    own_block = proj_grad_s[me]
    cot_block = cot_s[:, pl.ds(pl.multiple_of(me * block, block), block)]
    for ref, side in ((send_ref, 1 - core), (keep_ref, core)):
        lanes = pl.ds(pl.multiple_of(side * half, half), half)
        uvqk_term = dot_tn(scaled_ref[:, lanes], own_block)
        for b in range(4):
            ref[b * half : (b + 1) * half, :] = uvqk_term[:, b * block : (b + 1) * block].astype(
                ref.dtype
            )
        out_term = dot_tn(gated_s[:, lanes], cot_block)
        ref[4 * half : 5 * half, :] = out_term.astype(ref.dtype)
    own_rows = pl.ds(pl.multiple_of(me * rows, rows), rows)
    own_gated_ref[...] = gated_s[own_rows, :]
    for part in range(4):
        own_grad_ref[part] = proj_grad_s[part, own_rows, :]


def rows_kernel(
    own_ref, own_cot_ref, in_gain_ref, out_w_ref, own_gated_ref, scaled_ref, output_ref, grad_ref
):
    wide = own_ref[...].astype(F32)
    normed, inv_in = normalize(wide)
    grad_normed = scaled_ref[...] * in_gain_ref[...]
    grad_input = own_cot_ref[...].astype(F32) + norm_backward(grad_normed, normed, inv_in)
    grad_ref[...] = grad_input.astype(BF)
    output_ref[...] = (wide + dot_nn(own_gated_ref[...], out_w_ref[...])).astype(BF)


def small_kernel(
    own_ref, uvqk_ref, own_grad_ref, diag_ref, gain_ref, onehot_ref, scaled_ref, small_ref
):
    rows, width = own_ref.shape
    heads, _, total = diag_ref.shape
    buckets, span = onehot_ref.shape
    me = lax.axis_index("seq")
    normed, _ = normalize(own_ref[...].astype(F32))
    grad_scaled = jnp.zeros((rows, width), F32)
    for part in range(4):
        grad_scaled = grad_scaled + dot_nt(
            own_grad_ref[part], uvqk_ref[:, part * width : (part + 1) * width]
        )
    grad_in_gain = jnp.sum(grad_scaled * normed, axis=0, keepdims=True)
    scaled_ref[...] = grad_scaled

    onehot = onehot_ref[...]
    bias_sums = []
    for h in range(heads):
        folded = jnp.concatenate([diag_ref[h], jnp.zeros((rows, span - total), F32)], axis=1)
        count = rows // 2
        while count >= 8:
            folded = folded[:count, :] + pltpu.roll(folded[count:, :], span - count, 1)
            count //= 2
        while count >= 1:
            folded = folded + pltpu.roll(pltpu.roll(folded, 8 - count, 0), span - count, 1)
            count //= 2
        bias_sums.append(folded[:1, :])
    bias_sums = jnp.concatenate(bias_sums + [jnp.zeros((8 - heads, span), F32)], axis=0)
    grad_bias = sum(dot_nt(part, onehot) for part in three_parts(bias_sums))[:heads, :]
    small = jnp.concatenate(
        [
            grad_bias,
            as_rows(grad_in_gain, 4),
            as_rows(gain_ref[...], 4),
            jnp.zeros((4, buckets), F32),
        ],
        axis=0,
    )
    row = lax.broadcasted_iota(jnp.int32, small.shape, 0)
    mine = (row == me) | ((row >= 4) & (row < 8)) | (row == 8 + me)
    small_ref[...] = jnp.where(mine, small, 0.0)


def after_core_kernel(keep_ref, got_ref, small_ref, own_ref, *others):
    half = keep_ref.shape[0] // 5
    part = half // 4
    index = square_index()
    for ref, step in zip((own_ref,) + others, STEPS):
        there = jnp.bitwise_xor(index, step)
        for b in range(5):
            place = pl.ds(pl.multiple_of(b * half + there * part, part), part)
            ref[b * part : (b + 1) * part, :] = (
                keep_ref[place, :] + got_ref[place, :].astype(F32)
            ).astype(ref.dtype)
        small = jnp.where(there == 0, small_ref[...], 0.0)
        ref[5 * part :, :] = small.astype(ref.dtype)


def square_sum_kernel(own_ref, one_ref, three_ref, two_ref, sum_ref):
    body = own_ref.shape[0] - 16
    got = lambda ref, place: ref[place, :].astype(F32)
    for place, own in (
        (slice(0, body), own_ref[:body, :]),
        (slice(body, None), own_ref[body:, :].astype(BF).astype(F32)),
    ):
        sum_ref[place, :] = (
            (own + got(two_ref, place)) + (got(one_ref, place) + got(three_ref, place))
        ).astype(BF)


def pair_sum_kernel(left_ref, right_ref, sum_ref):
    sum_ref[...] = (left_ref[...].astype(F32) + right_ref[...].astype(F32)).astype(BF)


def four_sum_kernel(own_ref, one_ref, three_ref, two_ref, sum_ref):
    sum_ref[...] = (
        (own_ref[...].astype(F32) + two_ref[...].astype(F32))
        + (one_ref[...].astype(F32) + three_ref[...].astype(F32))
    ).astype(BF)


def join_kernel(*refs):
    joined = refs[-1]
    size = refs[0].shape[0]
    for n, ref in enumerate(refs[:-1]):
        joined[n * size : (n + 1) * size, :] = ref[...]


def unpack(factor, sources, kept, *refs):
    blocks = refs[: len(sources)]
    uvqk_hbm, out_hbm, wide_s, narrow_s, sems = refs[len(sources) + kept :]
    size = blocks[0].shape[0] // 4
    part = (size - 16) // 5
    width = uvqk_hbm.shape[1] // 4
    block = width // 4
    batch = lax.axis_index("batch")
    core = lax.rem(batch, 2)
    x = lax.axis_index("seq")
    index = square_index()
    copies = []
    for n, (ref, (other, second)) in enumerate(zip(blocks, sources)):
        from_core = 1 - core if other else core
        x_first = from_core == 1
        for m, first in enumerate(STEPS):
            slot = n * 4 + m
            from_x = lax.rem(x + 4 - jnp.where(x_first, first, second), 4)
            from_index = jnp.bitwise_xor(index, jnp.where(x_first, second, first))
            start = m * size
            for b in range(4):
                wide_s[slot, :, b * block : (b + 1) * block] = (
                    ref[start + b * part : start + (b + 1) * part, :].astype(F32) * factor
                )
            narrow_s[slot] = ref[start + 4 * part : start + 5 * part, :].astype(F32) * factor
            place = pl.ds(pl.multiple_of((from_core * 4 + from_index) * part, part), part)
            for copy in (
                pltpu.make_async_copy(
                    wide_s.at[slot],
                    uvqk_hbm.at[place, pl.ds(pl.multiple_of(from_x * width, width), width)],
                    sems.at[slot, 0],
                ),
                pltpu.make_async_copy(
                    narrow_s.at[slot],
                    out_hbm.at[place, pl.ds(pl.multiple_of(from_x * block, block), block)],
                    sems.at[slot, 1],
                ),
            ):
                copy.start()
                copies.append(copy)
    return copies


def unpack_kernel(factor, sources, kept, *refs):
    for copy in unpack(factor, sources, kept, *refs):
        copy.wait()


def last_kernel(factor, sources, kept, *refs):
    blocks = refs[:8]
    unpacked = refs[8 - len(sources) : 8 + kept]
    uvqk_hbm, out_hbm, *small_hbm = refs[8 + kept : 13 + kept]
    *scratch, small_s, small_sems = refs[13 + kept :]
    copies = unpack(factor, sources, kept, *unpacked, uvqk_hbm, out_hbm, *scratch)
    size = blocks[0].shape[0] // 4
    core = lax.rem(lax.axis_index("batch"), 2)

    def piece(ref, first):
        return ref[(first + 1) * size - 16 : (first + 1) * size, :].astype(F32)

    def over_x(own, x_first):
        by_first = [sum(piece(ref, n) for ref in own) for n in range(4)]
        by_second = [sum(piece(ref, n) for n in range(4)) for ref in own]
        zero, one, three, two = [
            jnp.where(x_first, left, right) for left, right in zip(by_first, by_second)
        ]
        return (zero + two) + (one + three)

    summed = (over_x(blocks[:4], core == 1) + over_x(blocks[4:], core == 0)) * factor
    for n, target in enumerate(small_hbm):
        small_s[n] = summed[4 * n : 4 * n + 4, :]
        copies.append(pltpu.make_async_copy(small_s.at[n], target, small_sems.at[n]))
        copies[-1].start()
    for copy in copies:
        copy.wait()


def params(limit):
    return pltpu.CompilerParams(vmem_limit_bytes=limit)


def cost(flops, bytes_accessed):
    return pl.CostEstimate(flops=flops, bytes_accessed=bytes_accessed, transcendentals=0)


def shards(
    history,
    out_cotangent,
    lengths,
    bucket_of,
    position_bias,
    norm_gain,
    uvqk_weight,
    out_gain,
    out_weight,
):
    rows, width = history.shape[1:]
    heads, buckets = position_bias.shape
    seq_size = lax.axis_size("seq")
    batch_size = lax.axis_size("batch")
    total = rows * seq_size
    span = total + rows
    z_size = batch_size // 8
    factor = 1.0 / math.sqrt(batch_size * total)

    def along_x(values, step):
        return lax.ppermute(values, "seq", [(i, (i + step) % seq_size) for i in range(seq_size)])

    def place_of(b):
        return b // (2 * z_size), (b // 2) % z_size, b % 2

    def along_batch(values, move):
        pairs = []
        for b in range(batch_size):
            y, z, c = move(*place_of(b))
            pairs.append((b, (y * z_size + z) * 2 + c))
        return lax.ppermute(values, "batch", pairs)

    def in_square(y, z, step):
        return y ^ (step // 2), z ^ (step % 2)

    def in_shifted_square(y, z, step):
        y, z = in_square(y + 1, z + 1, step)
        return (y - 1) % 4, (z - 1) % z_size

    def far(z):
        return (z + (5 if z % 2 else 3)) % z_size

    def across(values):
        return along_batch(values, lambda y, z, c: (y, z, 1 - c))

    def along_either(values, step, x_core):
        pairs = []
        for x in range(seq_size):
            for b in range(batch_size):
                y, z, c = place_of(b)
                to_x, to_y, to_z = x, y, z
                if c == x_core:
                    to_x = (x + step) % 4
                else:
                    to_y, to_z = in_square(y, z, step)
                pairs.append(
                    (x * batch_size + b, to_x * batch_size + (to_y * z_size + to_z) * 2 + c)
                )
        return lax.ppermute(values, ("seq", "batch"), pairs)

    shape = jax.ShapeDtypeStruct
    vmem = pl.BlockSpec(memory_space=pltpu.VMEM)
    smem = pl.BlockSpec(memory_space=pltpu.SMEM)
    hbm = pl.BlockSpec(memory_space=pltpu.HBM)
    own_history = history[0]
    own_cotangent = out_cotangent[0]
    pieces = [along_x(own_history, step) for step in STEPS[1:]]
    own, own_cot, in_gain, gain, uvqk, out_w, tile, onehot = pl.pallas_call(
        prepare_kernel,
        out_shape=[
            shape((rows, width), BF),
            shape((rows, width), BF),
            shape((1, width), F32),
            shape((1, width), F32),
            shape(uvqk_weight.shape, BF),
            shape(out_weight.shape, BF),
            shape((heads, rows, total), F32),
            shape((buckets, span), BF),
        ],
        in_specs=[hbm] * 8,
        out_specs=[vmem] * 8,
        scratch_shapes=[
            pltpu.VMEM((1, total), jnp.int32),
            pltpu.VMEM((heads, buckets), F32),
            pltpu.SemaphoreType.DMA((8,)),
        ],
        compiler_params=params(SMALL),
        cost_estimate=cost(10**9, 3 * 10**6),
        name="prepare",
    )(
        *[
            pltpu.with_memory_space_constraint(values, pltpu.HBM)
            for values in (
                bucket_of.reshape(1, total),
                position_bias,
                own_history,
                own_cotangent,
                norm_gain.reshape(1, width),
                out_gain.reshape(1, width),
                uvqk_weight,
                out_weight,
            )
        ]
    )
    cot_pieces = [along_x(own_cot, step) for step in STEPS[1:]]
    scaled, gate, slope, vqk, weights, score_slope, mixed = pl.pallas_call(
        functools.partial(forward_kernel, seq_size),
        out_shape=[
            shape((total, width), BF),
            shape((total, width), F32),
            shape((4, total, width), F32),
            shape((3, total, width), BF),
            shape((heads, total, total), BF),
            shape((heads, total, total), F32),
            shape((total, width), F32),
        ],
        scratch_shapes=[pltpu.VMEM((total, width), BF)],
        compiler_params=params(LARGE),
        cost_estimate=cost(4 * 10**9, 10**7),
        name="forward",
    )(own, *pieces, tile, in_gain, uvqk)
    half = total // 2
    body = 5 * half
    send, keep, own_gated, own_grad, diag, gain_term = pl.pallas_call(
        functools.partial(backward_kernel, seq_size),
        out_shape=[
            shape((body, buckets), BF),
            shape((body, buckets), F32),
            shape((rows, width), BF),
            shape((4, rows, width), BF),
            shape((heads, rows, total), F32),
            shape((1, width), F32),
        ],
        in_specs=[smem] + [vmem] * 13,
        out_specs=[vmem] * 6,
        scratch_shapes=[
            pltpu.VMEM((total, width), BF),
            pltpu.VMEM((total, width), BF),
            pltpu.VMEM((heads, total, total), BF),
            pltpu.VMEM((total, width), BF),
            pltpu.VMEM((4, total, width), BF),
            pltpu.VMEM((total, width), F32),
        ],
        compiler_params=params(LARGE),
        cost_estimate=cost(4 * 10**9, 10**7),
        name="backward",
    )(
        lengths,
        own_cot,
        *cot_pieces,
        gain,
        out_w,
        scaled,
        gate,
        slope,
        vqk,
        weights,
        score_slope,
        mixed,
    )

    got = across(send)
    grad_scaled, small = pl.pallas_call(
        small_kernel,
        out_shape=[shape((rows, width), F32), shape((16, buckets), F32)],
        compiler_params=params(SMALL),
        cost_estimate=cost(10**9, 3 * 10**6),
        name="small",
    )(own, uvqk, own_grad, diag, gain_term, onehot)

    part = half // 4
    size = 5 * part + 16
    chunk = (size, buckets)
    mine, *parts = pl.pallas_call(
        after_core_kernel,
        out_shape=[shape(chunk, F32)] + [shape(chunk, BF)] * 3,
        compiler_params=params(SMALL),
        name="after_core",
    )(keep, got, small)
    grad_scaled, mine, *parts = lax.optimization_barrier((grad_scaled, mine, *parts))
    output, grad_input = pl.pallas_call(
        rows_kernel,
        out_shape=[shape((rows, width), BF), shape((rows, width), BF)],
        compiler_params=params(SMALL),
        cost_estimate=cost(2 * 10**9, 3 * 10**6),
        name="rows",
    )(own, own_cot, in_gain, out_w, own_gated, grad_scaled)
    parts = [
        along_batch(values, lambda y, z, c: (*in_square(y, z, step), c))
        for values, step in zip(parts, STEPS[1:])
    ]
    summed = pl.pallas_call(
        square_sum_kernel,
        out_shape=shape(chunk, BF),
        compiler_params=params(SMALL),
        name="square_sum",
    )(mine, *parts)
    parts = [
        along_batch(summed, lambda y, z, c: (*in_shifted_square(y, z, step), c))
        for step in STEPS[1:]
    ]
    summed = pl.pallas_call(
        four_sum_kernel, out_shape=shape(chunk, BF), compiler_params=params(SMALL), name="four_sum"
    )(summed, *parts)
    other = along_batch(summed, lambda y, z, c: (y, far(z), c))
    summed = pl.pallas_call(
        pair_sum_kernel, out_shape=shape(chunk, BF), compiler_params=params(SMALL), name="pair_sum"
    )(summed, other)

    blocks = [along_either(summed, step, 1) for step in STEPS[1:]]
    joined = pl.pallas_call(
        join_kernel,
        out_shape=shape((4 * size, buckets), BF),
        compiler_params=params(SMALL),
        name="join",
    )(summed, *blocks)
    columns, others = {0: joined}, {}
    def unpack_call(sources, kept, last=False):
        blocks = [(others if other else columns)[step] for other, step in sources]
        slots = 4 * len(blocks)
        outs = [shape((width, 4 * width), F32), shape((width, width), F32)]
        if last:
            blocks = [columns[step] for step in STEPS] + [others[step] for step in STEPS]
        count = len(blocks)
        return pl.pallas_call(
            functools.partial(last_kernel if last else unpack_kernel, factor, sources, len(kept)),
            out_shape=outs + [shape((4, buckets), F32)] * (3 if last else 0),
            in_specs=[vmem] * count + [hbm] * len(kept),
            out_specs=[hbm] * (5 if last else 2),
            input_output_aliases={count + n: n for n in range(len(kept))},
            scratch_shapes=[
                pltpu.VMEM((slots, part, width), F32),
                pltpu.VMEM((slots, part, buckets), F32),
                pltpu.SemaphoreType.DMA((slots, 2)),
            ]
            + ([pltpu.VMEM((3, 4, buckets), F32), pltpu.SemaphoreType.DMA((3,))] if last else []),
            compiler_params=params(SMALL),
            cost_estimate=cost(UNPACK_FLOPS, 10**6 * slots // 4),
            name="unpack",
        )(*blocks, *kept)

    moved = {step: along_either(joined, step, 0) for step in STEPS[1:]}
    kept = unpack_call(((False, 0),), ())
    again, kept = lax.optimization_barrier((joined, kept))
    others[0] = across(again)
    for step in STEPS[1:]:
        columns[step], kept = lax.optimization_barrier((moved[step], kept))
        others[step] = across(columns[step])
    kept = unpack_call(((True, 0), (False, 1), (False, 3), (False, 2)), kept)
    grad_uvqk, grad_out_weight, grad_bias, grad_in_gain, grad_out_gain = unpack_call(
        ((True, 1), (True, 3), (True, 2)), kept, last=True
    )
    return (
        output[None],
        grad_input[None],
        grad_uvqk,
        grad_out_weight,
        grad_bias,
        grad_in_gain.reshape(width),
        grad_out_gain.reshape(width),
    )


def solution(mesh):
    return jax.shard_map(
        shards,
        mesh=mesh,
        in_specs=(
            P("batch", "seq", None),
            P("batch", "seq", None),
            P("batch"),
            P(),
            P(),
            P(),
            P(),
            P(),
            P(),
        ),
        out_specs=(P("batch", "seq", None), P("batch", "seq", None), P(), P(), P(), P(), P()),
        check_vma=False,
    )
```

```python
import functools
import math

import jax
import jax.numpy as jnp
from jax import lax
from jax.experimental import pallas as pl
from jax.experimental.pallas import tpu as pltpu
from jax.sharding import PartitionSpec as P

NORM_EPS = 1e-05
BF = jnp.bfloat16
F32 = jnp.float32
LARGE = 30 * 1024 * 1024
SMALL = 12 * 1024 * 1024
STEPS = (0, 1, 3, 2)
UNPACK_FLOPS = 10**10
FORWARD_GROUP = 4
BACKWARD_GROUP = 4
KEYS = 2
HIDDEN = -1e9


def normalize(values):
    centered = values - jnp.mean(values, axis=-1, keepdims=True)
    inv_scale = lax.rsqrt(jnp.mean(centered * centered, axis=-1, keepdims=True) + NORM_EPS)
    return (centered * inv_scale, inv_scale)


def norm_backward(grad_normed, normed, inv_scale):
    return inv_scale * (
        grad_normed
        - jnp.mean(grad_normed, axis=-1, keepdims=True)
        - normed * jnp.mean(grad_normed * normed, axis=-1, keepdims=True)
    )


def sigmoid(values):
    return 0.5 * jnp.tanh(0.5 * values) + 0.5


def dot_nn(left, right):
    return lax.dot_general(left, right, (((1,), (0,)), ((), ())), preferred_element_type=F32)


def dot_nt(left, right):
    return lax.dot_general(left, right, (((1,), (1,)), ((), ())), preferred_element_type=F32)


def dot_tn(left, right):
    return lax.dot_general(left, right, (((0,), (0,)), ((), ())), preferred_element_type=F32)


def three_parts(values):
    high = values.astype(BF)
    rest = values - high.astype(F32)
    middle = rest.astype(BF)
    low = (rest - middle.astype(F32)).astype(BF)
    return high, middle, low


def as_rows(row, parts):
    width = row.shape[1] // parts
    return jnp.concatenate([row[:, p * width : (p + 1) * width] for p in range(parts)], axis=0)


def prepare_kernel(
    bucket_hbm,
    bias_hbm,
    history_hbm,
    cotangent_hbm,
    in_gain_hbm,
    out_gain_hbm,
    uvqk_hbm,
    out_w_hbm,
    own_ref,
    own_cot_ref,
    in_gain_ref,
    out_gain_ref,
    uvqk_ref,
    out_w_ref,
    tile_ref,
    onehot_ref,
    bucket_ref,
    bias_ref,
    sems,
):
    copies = [
        pltpu.make_async_copy(source, target, sems.at[n])
        for n, (source, target) in enumerate(
            (
                (bucket_hbm, bucket_ref),
                (bias_hbm, bias_ref),
                (history_hbm, own_ref),
                (in_gain_hbm, in_gain_ref),
                (uvqk_hbm, uvqk_ref),
                (cotangent_hbm, own_cot_ref),
                (out_gain_hbm, out_gain_ref),
                (out_w_hbm, out_w_ref),
            )
        )
    ]
    for copy in copies:
        copy.start()
    heads, buckets = bias_ref.shape
    rows = own_ref.shape[0]
    total = bucket_ref.shape[1]
    copies[0].wait()
    copies[1].wait()

    span = total + rows
    offset = total - rows
    turned = offset - lax.broadcasted_iota(jnp.int32, (total, span), 1)
    turned = jnp.where(turned < 0, turned + span, turned)
    pick = (lax.broadcasted_iota(jnp.int32, (total, span), 0) == turned).astype(F32).astype(BF)
    bucket_rows = jnp.broadcast_to(bucket_ref[...].astype(F32), (8, total)).astype(BF)
    bucket_row = dot_nn(bucket_rows, pick)[:1, :]
    column = offset - lax.broadcasted_iota(jnp.int32, (1, span), 1)
    seen = jnp.where(column < 0, column + span, column) < total
    bucket_row = jnp.where(seen, bucket_row, -1.0)
    onehot = (
        lax.broadcasted_iota(jnp.int32, (buckets, span), 0).astype(F32)
        == jnp.broadcast_to(bucket_row, (buckets, span))
    ).astype(F32).astype(BF)
    onehot_ref[...] = onehot
    bias_rows = jnp.concatenate([bias_ref[...], jnp.zeros((8 - heads, buckets), F32)], axis=0)
    by_distance = sum(dot_nn(part, onehot) for part in three_parts(bias_rows))
    by_distance = jnp.where(seen, by_distance, HIDDEN)
    for h in range(heads):
        skewed = pltpu.roll(
            jnp.broadcast_to(by_distance[h : h + 1, :], (rows, span)), 0, 1, stride=1, stride_axis=0
        )
        tile_ref[h] = skewed[:, :total]
    for copy in copies[2:]:
        copy.wait()


def square_index():
    batch = lax.axis_index("batch")
    z_size = lax.axis_size("batch") // 8
    y = batch // (2 * z_size)
    z = lax.rem(batch // 2, z_size)
    bit = lambda place: lax.rem((place + 1) // 2, 2)
    return 2 * bit(y) + bit(z)


def place_pieces(refs, target, size):
    me = lax.axis_index("seq")
    for step, ref in zip(STEPS, refs):
        source = lax.rem(me + size - step, size)
        rows = ref.shape[0]
        target[pl.ds(pl.multiple_of(source * rows, rows), rows), :] = ref[...]


def forward_kernel(size, *refs):
    pieces = refs[:size]
    (
        tile_ref,
        in_gain_ref,
        uvqk_ref,
        scaled_ref,
        gate_ref,
        slope_ref,
        vqk_ref,
        weights_ref,
        score_slope_ref,
        mixed_ref,
        hist_s,
    ) = refs[size:]
    rows, width = pieces[0].shape
    total = rows * size
    heads = tile_ref.shape[0]
    head_dim = width // heads
    scale = 1.0 / math.sqrt(head_dim)
    in_gain = in_gain_ref[...]
    place_pieces(pieces, hist_s, size)
    normed, _ = normalize(hist_s[...].astype(F32))
    scaled_ref[...] = (normed * in_gain).astype(BF)
    for part in (2, 3, 1, 0):
        projected = dot_nn(scaled_ref[...], uvqk_ref[:, part * width : (part + 1) * width])
        sig = sigmoid(projected)
        activated = projected * sig
        slope_ref[part] = sig + activated * (1.0 - sig)
        if part == 0:
            gate_ref[...] = activated
        else:
            vqk_ref[part - 1] = activated.astype(BF)
    for i in range(0, size, FORWARD_GROUP):
        here = slice(i * rows, (i + FORWARD_GROUP) * rows)
        ends = (i + FORWARD_GROUP) * rows
        for h in range(heads):
            lanes = slice(h * head_dim, (h + 1) * head_dim)
            raw = dot_nt(vqk_ref[1, here, lanes], vqk_ref[2, :ends, lanes])
            for n in range(FORWARD_GROUP):
                block = slice((i + n) * rows, (i + n + 1) * rows)
                seen = (i + n + 1) * rows
                scores = raw[n * rows : (n + 1) * rows, :seen] * scale
                scores = scores + tile_ref[h, :, total - seen :]
                sig = sigmoid(scores)
                weights = scores * sig
                score_slope_ref[h, block, :seen] = sig + weights * (1.0 - sig)
                weights_ref[h, block, :seen] = weights.astype(BF)
                if n < FORWARD_GROUP - 1:
                    weights_ref[h, block, seen:ends] = jnp.zeros((rows, ends - seen), BF)
            mixed_ref[here, lanes] = dot_nn(weights_ref[h, here, :ends], vqk_ref[0, :ends, lanes])


def backward_kernel(size, length_ref, *refs):
    pieces = refs[:size]
    (
        out_gain_ref,
        out_w_ref,
        scaled_ref,
        gate_ref,
        slope_ref,
        vqk_ref,
        weights_ref,
        score_slope_ref,
        mixed_ref,
        send_ref,
        keep_ref,
        own_gated_ref,
        own_grad_ref,
        diag_ref,
        gain_ref,
        cot_s,
        gated_s,
        grads_s,
        grad_mixed_s,
        proj_grad_s,
        grad_gated_s,
    ) = refs[size:]
    rows, width = pieces[0].shape
    total = rows * size
    heads = weights_ref.shape[0]
    head_dim = width // heads
    scale = 1.0 / math.sqrt(head_dim)
    me = lax.axis_index("seq")
    core = lax.rem(lax.axis_index("batch"), 2)
    length = length_ref[0]
    out_gain = out_gain_ref[...]
    place_pieces(pieces, cot_s, size)
    grad_out_gain = jnp.zeros((1, width), F32)
    for h in range(heads):
        diag_ref[h] = jnp.zeros((rows, total), F32)
    grad_gated_s[...] = dot_nt(cot_s[...], out_w_ref[...])
    for i in range(0, size, BACKWARD_GROUP):
        here = slice(i * rows, (i + BACKWARD_GROUP) * rows)
        ends = (i + BACKWARD_GROUP) * rows
        valid = (lax.broadcasted_iota(jnp.int32, (BACKWARD_GROUP * rows, 1), 0) + i * rows) < length
        mixed = jnp.where(valid, mixed_ref[here, :], 0.0)
        mixed_normed, inv_mixed = normalize(mixed)
        gating = gate_ref[here, :]
        gated_s[here, :] = (mixed_normed * out_gain * gating).astype(BF)
        grad_gated = grad_gated_s[here, :]
        times_normed = grad_gated * mixed_normed
        grad_out_gain = grad_out_gain + jnp.sum(times_normed * gating, axis=0, keepdims=True)
        proj_grad_s[0, here, :] = (times_normed * out_gain * slope_ref[0, here, :]).astype(BF)
        grad_mixed = norm_backward(grad_gated * out_gain * gating, mixed_normed, inv_mixed)
        grad_mixed_s[here, :] = jnp.where(valid, grad_mixed, 0.0).astype(BF)
        by_head = [slice(h * head_dim, (h + 1) * head_dim) for h in range(heads)]
        products = [dot_nt(grad_mixed_s[here, lanes], vqk_ref[0, :ends, lanes]) for lanes in by_head]
        for h, grad_weights in enumerate(products):
            for n in range(BACKWARD_GROUP):
                block = slice((i + n) * rows, (i + n + 1) * rows)
                seen = (i + n + 1) * rows
                grad_scores = (
                    grad_weights[n * rows : (n + 1) * rows, :seen] * score_slope_ref[h, block, :seen]
                )
                diag_ref[h, :, total - seen :] += grad_scores
                grads_s[h, block, :seen] = grad_scores.astype(BF)
                if n < BACKWARD_GROUP - 1:
                    grads_s[h, block, seen:ends] = jnp.zeros((rows, ends - seen), BF)
        for h, lanes in enumerate(by_head):
            grad_query = dot_nn(grads_s[h, here, :ends], vqk_ref[2, :ends, lanes]) * scale
            proj_grad_s[2, here, lanes] = (grad_query * slope_ref[2, here, lanes]).astype(BF)
    gain_ref[...] = grad_out_gain

    for j in range(0, size, KEYS):
        here = slice(j * rows, (j + KEYS) * rows)
        later = slice(j * rows, total)
        for h in range(heads):
            lanes = slice(h * head_dim, (h + 1) * head_dim)
            grad_key = dot_tn(grads_s[h, later, here], vqk_ref[1, later, lanes]) * scale
            proj_grad_s[3, here, lanes] = (grad_key * slope_ref[3, here, lanes]).astype(BF)
            grad_value = dot_tn(weights_ref[h, later, here], grad_mixed_s[later, lanes])
            proj_grad_s[1, here, lanes] = (grad_value * slope_ref[1, here, lanes]).astype(BF)

    half = total // 2
    block = width // 4
    own_block = proj_grad_s[me]
    cot_block = cot_s[:, pl.ds(pl.multiple_of(me * block, block), block)]
    for ref, side in ((send_ref, 1 - core), (keep_ref, core)):
        lanes = pl.ds(pl.multiple_of(side * half, half), half)
        uvqk_term = dot_tn(scaled_ref[:, lanes], own_block)
        for b in range(4):
            ref[b * half : (b + 1) * half, :] = uvqk_term[:, b * block : (b + 1) * block].astype(
                ref.dtype
            )
        out_term = dot_tn(gated_s[:, lanes], cot_block)
        ref[4 * half : 5 * half, :] = out_term.astype(ref.dtype)
    own_rows = pl.ds(pl.multiple_of(me * rows, rows), rows)
    own_gated_ref[...] = gated_s[own_rows, :]
    for part in range(4):
        own_grad_ref[part] = proj_grad_s[part, own_rows, :]


def rows_kernel(
    own_ref, own_cot_ref, in_gain_ref, out_w_ref, own_gated_ref, scaled_ref, output_ref, grad_ref
):
    wide = own_ref[...].astype(F32)
    normed, inv_in = normalize(wide)
    grad_normed = scaled_ref[...] * in_gain_ref[...]
    grad_input = own_cot_ref[...].astype(F32) + norm_backward(grad_normed, normed, inv_in)
    grad_ref[...] = grad_input.astype(BF)
    output_ref[...] = (wide + dot_nn(own_gated_ref[...], out_w_ref[...])).astype(BF)


def small_kernel(
    own_ref, uvqk_ref, own_grad_ref, diag_ref, gain_ref, onehot_ref, scaled_ref, small_ref
):
    rows, width = own_ref.shape
    heads, _, total = diag_ref.shape
    buckets, span = onehot_ref.shape
    me = lax.axis_index("seq")
    normed, _ = normalize(own_ref[...].astype(F32))
    grad_scaled = jnp.zeros((rows, width), F32)
    for part in range(4):
        grad_scaled = grad_scaled + dot_nt(
            own_grad_ref[part], uvqk_ref[:, part * width : (part + 1) * width]
        )
    grad_in_gain = jnp.sum(grad_scaled * normed, axis=0, keepdims=True)
    scaled_ref[...] = grad_scaled

    onehot = onehot_ref[...]
    bias_sums = []
    for h in range(heads):
        folded = jnp.concatenate([diag_ref[h], jnp.zeros((rows, span - total), F32)], axis=1)
        count = rows // 2
        while count >= 8:
            folded = folded[:count, :] + pltpu.roll(folded[count:, :], span - count, 1)
            count //= 2
        while count >= 1:
            folded = folded + pltpu.roll(pltpu.roll(folded, 8 - count, 0), span - count, 1)
            count //= 2
        bias_sums.append(folded[:1, :])
    bias_sums = jnp.concatenate(bias_sums + [jnp.zeros((8 - heads, span), F32)], axis=0)
    grad_bias = sum(dot_nt(part, onehot) for part in three_parts(bias_sums))[:heads, :]
    small = jnp.concatenate(
        [
            grad_bias,
            as_rows(grad_in_gain, 4),
            as_rows(gain_ref[...], 4),
            jnp.zeros((4, buckets), F32),
        ],
        axis=0,
    )
    row = lax.broadcasted_iota(jnp.int32, small.shape, 0)
    mine = (row == me) | ((row >= 4) & (row < 8)) | (row == 8 + me)
    small_ref[...] = jnp.where(mine, small, 0.0)


def after_core_kernel(keep_ref, got_ref, small_ref, own_ref, *others):
    half = keep_ref.shape[0] // 5
    part = half // 4
    index = square_index()
    for ref, step in zip((own_ref,) + others, STEPS):
        there = jnp.bitwise_xor(index, step)
        for b in range(5):
            place = pl.ds(pl.multiple_of(b * half + there * part, part), part)
            ref[b * part : (b + 1) * part, :] = (
                keep_ref[place, :] + got_ref[place, :].astype(F32)
            ).astype(ref.dtype)
        small = jnp.where(there == 0, small_ref[...], 0.0)
        ref[5 * part :, :] = small.astype(ref.dtype)


def square_sum_kernel(own_ref, one_ref, three_ref, two_ref, sum_ref):
    body = own_ref.shape[0] - 16
    got = lambda ref, place: ref[place, :].astype(F32)
    for place, own in (
        (slice(0, body), own_ref[:body, :]),
        (slice(body, None), own_ref[body:, :].astype(BF).astype(F32)),
    ):
        sum_ref[place, :] = (
            (own + got(two_ref, place)) + (got(one_ref, place) + got(three_ref, place))
        ).astype(BF)


def pair_sum_kernel(left_ref, right_ref, sum_ref):
    sum_ref[...] = (left_ref[...].astype(F32) + right_ref[...].astype(F32)).astype(BF)


def four_sum_kernel(own_ref, one_ref, three_ref, two_ref, sum_ref):
    sum_ref[...] = (
        (own_ref[...].astype(F32) + two_ref[...].astype(F32))
        + (one_ref[...].astype(F32) + three_ref[...].astype(F32))
    ).astype(BF)


def join_kernel(*refs):
    joined = refs[-1]
    size = refs[0].shape[0]
    for n, ref in enumerate(refs[:-1]):
        joined[n * size : (n + 1) * size, :] = ref[...]


def unpack(factor, sources, kept, *refs):
    blocks = refs[: len(sources)]
    uvqk_hbm, out_hbm, wide_s, narrow_s, sems = refs[len(sources) + kept :]
    size = blocks[0].shape[0] // 4
    part = (size - 16) // 5
    width = uvqk_hbm.shape[1] // 4
    block = width // 4
    batch = lax.axis_index("batch")
    core = lax.rem(batch, 2)
    x = lax.axis_index("seq")
    index = square_index()
    copies = []
    for n, (ref, (other, second)) in enumerate(zip(blocks, sources)):
        from_core = 1 - core if other else core
        x_first = from_core == 1
        for m, first in enumerate(STEPS):
            slot = n * 4 + m
            from_x = lax.rem(x + 4 - jnp.where(x_first, first, second), 4)
            from_index = jnp.bitwise_xor(index, jnp.where(x_first, second, first))
            start = m * size
            for b in range(4):
                wide_s[slot, :, b * block : (b + 1) * block] = (
                    ref[start + b * part : start + (b + 1) * part, :].astype(F32) * factor
                )
            narrow_s[slot] = ref[start + 4 * part : start + 5 * part, :].astype(F32) * factor
            place = pl.ds(pl.multiple_of((from_core * 4 + from_index) * part, part), part)
            for copy in (
                pltpu.make_async_copy(
                    wide_s.at[slot],
                    uvqk_hbm.at[place, pl.ds(pl.multiple_of(from_x * width, width), width)],
                    sems.at[slot, 0],
                ),
                pltpu.make_async_copy(
                    narrow_s.at[slot],
                    out_hbm.at[place, pl.ds(pl.multiple_of(from_x * block, block), block)],
                    sems.at[slot, 1],
                ),
            ):
                copy.start()
                copies.append(copy)
    return copies


def unpack_kernel(factor, sources, kept, *refs):
    for copy in unpack(factor, sources, kept, *refs):
        copy.wait()


def last_kernel(factor, sources, kept, *refs):
    blocks = refs[:8]
    unpacked = refs[8 - len(sources) : 8 + kept]
    uvqk_hbm, out_hbm, *small_hbm = refs[8 + kept : 13 + kept]
    *scratch, small_s, small_sems = refs[13 + kept :]
    copies = unpack(factor, sources, kept, *unpacked, uvqk_hbm, out_hbm, *scratch)
    size = blocks[0].shape[0] // 4
    core = lax.rem(lax.axis_index("batch"), 2)

    def piece(ref, first):
        return ref[(first + 1) * size - 16 : (first + 1) * size, :].astype(F32)

    def over_x(own, x_first):
        by_first = [sum(piece(ref, n) for ref in own) for n in range(4)]
        by_second = [sum(piece(ref, n) for n in range(4)) for ref in own]
        zero, one, three, two = [
            jnp.where(x_first, left, right) for left, right in zip(by_first, by_second)
        ]
        return (zero + two) + (one + three)

    summed = (over_x(blocks[:4], core == 1) + over_x(blocks[4:], core == 0)) * factor
    for n, target in enumerate(small_hbm):
        small_s[n] = summed[4 * n : 4 * n + 4, :]
        copies.append(pltpu.make_async_copy(small_s.at[n], target, small_sems.at[n]))
        copies[-1].start()
    for copy in copies:
        copy.wait()


def params(limit):
    return pltpu.CompilerParams(vmem_limit_bytes=limit)


def cost(flops, bytes_accessed):
    return pl.CostEstimate(flops=flops, bytes_accessed=bytes_accessed, transcendentals=0)


def shards(
    history,
    out_cotangent,
    lengths,
    bucket_of,
    position_bias,
    norm_gain,
    uvqk_weight,
    out_gain,
    out_weight,
):
    rows, width = history.shape[1:]
    heads, buckets = position_bias.shape
    seq_size = lax.axis_size("seq")
    batch_size = lax.axis_size("batch")
    total = rows * seq_size
    span = total + rows
    z_size = batch_size // 8
    factor = 1.0 / math.sqrt(batch_size * total)

    def along_x(values, step):
        return lax.ppermute(values, "seq", [(i, (i + step) % seq_size) for i in range(seq_size)])

    def place_of(b):
        return b // (2 * z_size), (b // 2) % z_size, b % 2

    def along_batch(values, move):
        pairs = []
        for b in range(batch_size):
            y, z, c = move(*place_of(b))
            pairs.append((b, (y * z_size + z) * 2 + c))
        return lax.ppermute(values, "batch", pairs)

    def in_square(y, z, step):
        return y ^ (step // 2), z ^ (step % 2)

    def in_shifted_square(y, z, step):
        y, z = in_square(y + 1, z + 1, step)
        return (y - 1) % 4, (z - 1) % z_size

    def far(z):
        return (z + (5 if z % 2 else 3)) % z_size

    def across(values):
        return along_batch(values, lambda y, z, c: (y, z, 1 - c))

    def along_either(values, step, x_core):
        pairs = []
        for x in range(seq_size):
            for b in range(batch_size):
                y, z, c = place_of(b)
                to_x, to_y, to_z = x, y, z
                if c == x_core:
                    to_x = (x + step) % 4
                else:
                    to_y, to_z = in_square(y, z, step)
                pairs.append(
                    (x * batch_size + b, to_x * batch_size + (to_y * z_size + to_z) * 2 + c)
                )
        return lax.ppermute(values, ("seq", "batch"), pairs)

    shape = jax.ShapeDtypeStruct
    vmem = pl.BlockSpec(memory_space=pltpu.VMEM)
    smem = pl.BlockSpec(memory_space=pltpu.SMEM)
    hbm = pl.BlockSpec(memory_space=pltpu.HBM)
    own_history = history[0]
    own_cotangent = out_cotangent[0]
    pieces = [along_x(own_history, step) for step in STEPS[1:]]
    own, own_cot, in_gain, gain, uvqk, out_w, tile, onehot = pl.pallas_call(
        prepare_kernel,
        out_shape=[
            shape((rows, width), BF),
            shape((rows, width), BF),
            shape((1, width), F32),
            shape((1, width), F32),
            shape(uvqk_weight.shape, BF),
            shape(out_weight.shape, BF),
            shape((heads, rows, total), F32),
            shape((buckets, span), BF),
        ],
        in_specs=[hbm] * 8,
        out_specs=[vmem] * 8,
        scratch_shapes=[
            pltpu.VMEM((1, total), jnp.int32),
            pltpu.VMEM((heads, buckets), F32),
            pltpu.SemaphoreType.DMA((8,)),
        ],
        compiler_params=params(SMALL),
        cost_estimate=cost(10**9, 3 * 10**6),
        name="prepare",
    )(
        *[
            pltpu.with_memory_space_constraint(values, pltpu.HBM)
            for values in (
                bucket_of.reshape(1, total),
                position_bias,
                own_history,
                own_cotangent,
                norm_gain.reshape(1, width),
                out_gain.reshape(1, width),
                uvqk_weight,
                out_weight,
            )
        ]
    )
    cot_pieces = [along_x(own_cot, step) for step in STEPS[1:]]
    scaled, gate, slope, vqk, weights, score_slope, mixed = pl.pallas_call(
        functools.partial(forward_kernel, seq_size),
        out_shape=[
            shape((total, width), BF),
            shape((total, width), F32),
            shape((4, total, width), F32),
            shape((3, total, width), BF),
            shape((heads, total, total), BF),
            shape((heads, total, total), F32),
            shape((total, width), F32),
        ],
        scratch_shapes=[pltpu.VMEM((total, width), BF)],
        compiler_params=params(LARGE),
        cost_estimate=cost(4 * 10**9, 10**7),
        name="forward",
    )(own, *pieces, tile, in_gain, uvqk)
    half = total // 2
    body = 5 * half
    send, keep, own_gated, own_grad, diag, gain_term = pl.pallas_call(
        functools.partial(backward_kernel, seq_size),
        out_shape=[
            shape((body, buckets), BF),
            shape((body, buckets), F32),
            shape((rows, width), BF),
            shape((4, rows, width), BF),
            shape((heads, rows, total), F32),
            shape((1, width), F32),
        ],
        in_specs=[smem] + [vmem] * 13,
        out_specs=[vmem] * 6,
        scratch_shapes=[
            pltpu.VMEM((total, width), BF),
            pltpu.VMEM((total, width), BF),
            pltpu.VMEM((heads, total, total), BF),
            pltpu.VMEM((total, width), BF),
            pltpu.VMEM((4, total, width), BF),
            pltpu.VMEM((total, width), F32),
        ],
        compiler_params=params(LARGE),
        cost_estimate=cost(4 * 10**9, 10**7),
        name="backward",
    )(
        lengths,
        own_cot,
        *cot_pieces,
        gain,
        out_w,
        scaled,
        gate,
        slope,
        vqk,
        weights,
        score_slope,
        mixed,
    )

    got = across(send)
    grad_scaled, small = pl.pallas_call(
        small_kernel,
        out_shape=[shape((rows, width), F32), shape((16, buckets), F32)],
        compiler_params=params(SMALL),
        cost_estimate=cost(10**9, 3 * 10**6),
        name="small",
    )(own, uvqk, own_grad, diag, gain_term, onehot)

    part = half // 4
    size = 5 * part + 16
    chunk = (size, buckets)
    mine, *parts = pl.pallas_call(
        after_core_kernel,
        out_shape=[shape(chunk, F32)] + [shape(chunk, BF)] * 3,
        compiler_params=params(SMALL),
        name="after_core",
    )(keep, got, small)
    grad_scaled, mine, *parts = lax.optimization_barrier((grad_scaled, mine, *parts))
    output, grad_input = pl.pallas_call(
        rows_kernel,
        out_shape=[shape((rows, width), BF), shape((rows, width), BF)],
        compiler_params=params(SMALL),
        cost_estimate=cost(2 * 10**9, 3 * 10**6),
        name="rows",
    )(own, own_cot, in_gain, out_w, own_gated, grad_scaled)
    parts = [
        along_batch(values, lambda y, z, c: (*in_square(y, z, step), c))
        for values, step in zip(parts, STEPS[1:])
    ]
    summed = pl.pallas_call(
        square_sum_kernel,
        out_shape=shape(chunk, BF),
        compiler_params=params(SMALL),
        name="square_sum",
    )(mine, *parts)
    parts = [
        along_batch(summed, lambda y, z, c: (*in_shifted_square(y, z, step), c))
        for step in STEPS[1:]
    ]
    summed = pl.pallas_call(
        four_sum_kernel, out_shape=shape(chunk, BF), compiler_params=params(SMALL), name="four_sum"
    )(summed, *parts)
    other = along_batch(summed, lambda y, z, c: (y, far(z), c))
    summed = pl.pallas_call(
        pair_sum_kernel, out_shape=shape(chunk, BF), compiler_params=params(SMALL), name="pair_sum"
    )(summed, other)

    blocks = [along_either(summed, step, 1) for step in STEPS[1:]]
    joined = pl.pallas_call(
        join_kernel,
        out_shape=shape((4 * size, buckets), BF),
        compiler_params=params(SMALL),
        name="join",
    )(summed, *blocks)
    columns, others = {0: joined}, {}
    def unpack_call(sources, kept, last=False):
        blocks = [(others if other else columns)[step] for other, step in sources]
        slots = 4 * len(blocks)
        outs = [shape((width, 4 * width), F32), shape((width, width), F32)]
        if last:
            blocks = [columns[step] for step in STEPS] + [others[step] for step in STEPS]
        count = len(blocks)
        return pl.pallas_call(
            functools.partial(last_kernel if last else unpack_kernel, factor, sources, len(kept)),
            out_shape=outs + [shape((4, buckets), F32)] * (3 if last else 0),
            in_specs=[vmem] * count + [hbm] * len(kept),
            out_specs=[hbm] * (5 if last else 2),
            input_output_aliases={count + n: n for n in range(len(kept))},
            scratch_shapes=[
                pltpu.VMEM((slots, part, width), F32),
                pltpu.VMEM((slots, part, buckets), F32),
                pltpu.SemaphoreType.DMA((slots, 2)),
            ]
            + ([pltpu.VMEM((3, 4, buckets), F32), pltpu.SemaphoreType.DMA((3,))] if last else []),
            compiler_params=params(SMALL),
            cost_estimate=cost(UNPACK_FLOPS, 10**6 * slots // 4),
            name="unpack",
        )(*blocks, *kept)

    moved = {step: along_either(joined, step, 0) for step in STEPS[1:]}
    others[0] = across(joined)
    kept = unpack_call(((False, 0), (True, 0)), ())
    for step in STEPS[1:]:
        columns[step], kept = lax.optimization_barrier((moved[step], kept))
        others[step] = across(columns[step])
    kept = unpack_call(((False, 1), (False, 3), (False, 2)), kept)
    grad_uvqk, grad_out_weight, grad_bias, grad_in_gain, grad_out_gain = unpack_call(
        ((True, 1), (True, 3), (True, 2)), kept, last=True
    )
    return (
        output[None],
        grad_input[None],
        grad_uvqk,
        grad_out_weight,
        grad_bias,
        grad_in_gain.reshape(width),
        grad_out_gain.reshape(width),
    )


def solution(mesh):
    return jax.shard_map(
        shards,
        mesh=mesh,
        in_specs=(
            P("batch", "seq", None),
            P("batch", "seq", None),
            P("batch"),
            P(),
            P(),
            P(),
            P(),
            P(),
            P(),
        ),
        out_specs=(P("batch", "seq", None), P("batch", "seq", None), P(), P(), P(), P(), P()),
        check_vma=False,
    )
```
